32 devices in a mesh: seq: 8 (over z, y), head: 4 (over x, core).
Axes of the slice: x: 2, y: 2, z: 4, core: 2. Of those that a mesh axis runs over, the one named last changes fastest.
Arguments:
- queries: bfloat16 [4096, 8192], P('seq', 'head'), may hold values from -6 to 6
- keys: bfloat16 [4096, 8192], P('seq', 'head'), may hold values from -0.52734375 to 0.52734375
- values: bfloat16 [4096, 8192], P('seq', 'head'), may hold values from -6 to 6
- suffix_keys: bfloat16 [32, 128, 8192], P('seq', None, 'head'), may hold values from -0.52734375 to 0.52734375
- suffix_values: bfloat16 [32, 128, 8192], P('seq', None, 'head'), may hold values from -6 to 6
- suffix_lengths: int32 [32], P('seq'), may hold values from 1 to 128
- step_queries: bfloat16 [2, 32, 8192], P(None, 'seq', 'head'), may hold values from -6 to 6
- step_keys: bfloat16 [2, 32, 8192], P(None, 'seq', 'head'), may hold values from -0.52734375 to 0.52734375
- step_values: bfloat16 [2, 32, 8192], P(None, 'seq', 'head'), may hold values from -6 to 6
- norm_gain: float32 [8192], P('head'), may hold values from 0.1 to 1.9
Outputs:
- prompt_out: bfloat16 [4096, 8192], P('seq', 'head')
- decoded: bfloat16 [2, 32, 8192], P(None, 'seq', 'head')
The draws below stay inside these ranges and needn't reach their ends.
All inputs are finite; a program needn't handle non-finite values.
Results may differ from the reference program's by a relative error of at most 0.005.
Values sent between devices are 32-bit elements; how exact they have to be, the bound alone decides.
No kernel may reach another device: no remote copies, remote signals or barrier semaphores. Data moves between devices by JAX's collectives and lax.ppermute only.
A program may use at most 128 MiB of HBM per device.

```python
import jax
import jax.numpy as jnp
from jax import lax

HEADS = 64
HEAD_DIM = 128
SPAN = 512
SUF = 128
STEPS = 2
WIDTH = 8192
PROMPT = 4096
SAMPLES = 32
N_SEQ = 8


def plant(result, rng, least, largest):
    spot = [jax.random.randint(jax.random.fold_in(rng, axis), (), 0, length) for axis, length in enumerate(result.shape)]
    main_axis = result.shape.index(max(result.shape))
    next_to = spot[:main_axis] + [(spot[main_axis] + 1) % result.shape[main_axis]] + spot[main_axis + 1:]
    return result.at[tuple(spot)].set(least).at[tuple(next_to)].set(largest)


def levels(key, extent, cuts, low, high):
    factor_of, own = 1.0, jax.random.fold_in(key, 6)
    for axis_at, shards_of in cuts:
        steps = jnp.exp(jax.random.uniform(jax.random.fold_in(own, axis_at), (shards_of,), jnp.float32, low / len(cuts), high / len(cuts)))
        factor_of = factor_of * jnp.repeat(steps, extent[axis_at] // shards_of).reshape([-1 if axis == axis_at else 1 for axis in range(len(extent))])
    return factor_of


def noise(rng, shape, width, limit, shards=(), held_as=jnp.bfloat16):
    loudness = levels(rng, shape, shards, -0.22, 0.18) if shards else 1.0
    values = jax.random.normal(rng, shape, jnp.float32) * width * loudness
    return jnp.minimum(jnp.maximum(values, -limit), limit).astype(held_as)


def setup_inputs(seed: int = 0) -> dict:
    arg_keys = jax.random.split(jax.random.key(seed), 11)
    queries = noise(arg_keys[0], (PROMPT, WIDTH), 1.0, 6.0, ((0, 8), (1, 4)))
    keys = noise(arg_keys[1], (PROMPT, WIDTH), 0.088, 0.52734375, ((0, 8), (1, 4)))
    values = noise(arg_keys[2], (PROMPT, WIDTH), 1.0, 6.0, ((0, 8), (1, 4)))
    suffix_keys = noise(arg_keys[3], (SAMPLES, SUF, WIDTH), 0.088, 0.52734375, ((0, 8), (2, 4)))
    suffix_values = noise(arg_keys[4], (SAMPLES, SUF, WIDTH), 1.0, 6.0, ((0, 8), (2, 4)))
    suffix_lengths = plant(jax.random.randint(arg_keys[5], (SAMPLES,), 1, SUF + 1), jax.random.fold_in(arg_keys[5], 1), 1, SUF).astype(jnp.int32)
    step_queries = noise(arg_keys[6], (STEPS, SAMPLES, WIDTH), 1.0, 6.0, ((1, 8), (2, 4)))
    step_keys = noise(arg_keys[7], (STEPS, SAMPLES, WIDTH), 0.088, 0.52734375, ((1, 8), (2, 4)))
    step_values = noise(arg_keys[8], (STEPS, SAMPLES, WIDTH), 1.0, 6.0, ((1, 8), (2, 4)))
    norm_gain = jnp.clip(1.0 + 0.18 * jax.random.normal(arg_keys[9], (WIDTH,), jnp.float32), 0.1, 1.9)
    return {"queries": queries, "keys": keys, "values": values, "suffix_keys": suffix_keys, "suffix_values": suffix_values, "suffix_lengths": suffix_lengths, "step_queries": step_queries, "step_keys": step_keys, "step_values": step_values, "norm_gain": norm_gain}


HIGHEST_PREC = lax.Precision.HIGHEST

def normalize(raw, norm_gain):
    mean_sq = lax.optimization_barrier(jnp.mean(raw * raw, axis=-1, keepdims=True))
    return (raw * lax.rsqrt(mean_sq + 1e-06) * norm_gain).astype(jnp.bfloat16)

def reference(queries, keys, values, suffix_keys, suffix_values, suffix_lengths, step_queries, step_keys, step_values, norm_gain):
    all_queries = queries.reshape(N_SEQ, SPAN, HEADS, HEAD_DIM).astype(jnp.float32)
    all_keys = keys.reshape(N_SEQ, SPAN, HEADS, HEAD_DIM).astype(jnp.float32)
    all_values = values.reshape(N_SEQ, SPAN, HEADS, HEAD_DIM).astype(jnp.float32)
    positions = jnp.arange(SPAN, dtype=jnp.int32)
    causal = positions[None, :] <= positions[:, None]

    def block_step(state, inputs):
        block_queries, block_keys, block_values = inputs
        scores = jnp.einsum('chd,shd->hcs', block_queries, block_keys, precision=HIGHEST_PREC)
        scores = jnp.where(causal[None], scores, 0.0).astype(jnp.bfloat16)
        scores = lax.optimization_barrier(scores).astype(jnp.float32)
        intra = jnp.einsum('hcs,she->che', scores, block_values, precision=HIGHEST_PREC)
        prior_low = lax.optimization_barrier(state.astype(jnp.bfloat16)).astype(jnp.float32)
        inter = jnp.einsum('chd,hde->che', block_queries, prior_low, precision=HIGHEST_PREC)
        attended = intra + inter
        new_state = state + jnp.einsum('chd,che->hde', block_keys, block_values, precision=HIGHEST_PREC)
        return (new_state, attended)
    zero = jnp.zeros((HEADS, HEAD_DIM, HEAD_DIM), jnp.float32)
    final, attended = lax.scan(block_step, zero, (all_queries, all_keys, all_values))
    prompt_out = normalize(attended.reshape(PROMPT, WIDTH), norm_gain)
    live = (jnp.arange(SUF, dtype=jnp.int32)[None, :] < suffix_lengths[:, None]).astype(jnp.float32)
    masked_keys = suffix_keys.reshape(SAMPLES, SUF, HEADS, HEAD_DIM).astype(jnp.float32) * live[:, :, None, None]
    suffix_vals = suffix_values.reshape(SAMPLES, SUF, HEADS, HEAD_DIM).astype(jnp.float32)
    state = final[None] + jnp.einsum('bjhd,bjhe->bhde', masked_keys, suffix_vals, precision=HIGHEST_PREC)
    outputs = []
    for step in range(STEPS):
        new_keys = step_keys[step].reshape(SAMPLES, HEADS, HEAD_DIM).astype(jnp.float32)
        new_vals = step_values[step].reshape(SAMPLES, HEADS, HEAD_DIM).astype(jnp.float32)
        new_query = step_queries[step].reshape(SAMPLES, HEADS, HEAD_DIM).astype(jnp.float32)
        state = state + jnp.einsum('bhd,bhe->bhde', new_keys, new_vals, precision=HIGHEST_PREC)
        raw = jnp.einsum('bhd,bhde->bhe', new_query, state, precision=HIGHEST_PREC)
        outputs.append(raw.reshape(SAMPLES, WIDTH))
    decoded = normalize(jnp.stack(outputs), norm_gain)
    return (prompt_out, decoded)
```

```python
import functools

import jax
import jax.numpy as jnp
from jax import lax
from jax.experimental import pallas as pl
from jax.experimental.pallas import tpu as pltpu
from jax.sharding import PartitionSpec as P

HEAD_DIM = 128
LANES = 128
CHUNKS = 2
F32 = jnp.float32
BF16 = jnp.bfloat16
VMEM_LIMIT = 48 * 1024 * 1024


def dot(a, b, contract=((1,), (0,))):
    return lax.dot_general(a, b, (contract, ((), ())), preferred_element_type=F32)


def params(semantics=None):
    return pltpu.CompilerParams(vmem_limit_bytes=VMEM_LIMIT, dimension_semantics=semantics)


def cost(flops, moved):
    return pl.CostEstimate(flops=int(flops), bytes_accessed=int(moved), transcendentals=0)


def head_cols(head):
    return slice(head * HEAD_DIM, (head + 1) * HEAD_DIM)


def flat_rows(ref):
    return jnp.concatenate([ref[i].astype(F32) for i in range(ref.shape[0])], axis=0)


def state_kernel(group, place_ref, k_ref, v_ref, q_ref, *out_refs):
    heads = out_refs[0].shape[0]
    turn = pl.program_id(0)
    for m in range(group):

        @pl.when(turn == m)
        def _():
            rows = flat_rows(q_ref)
            for h in range(heads):
                cols = head_cols(h)
                out_refs[m][h, :HEAD_DIM, :] = dot(k_ref[:, cols], v_ref[:, cols], ((0,), (0,)))
                out_refs[m][h, HEAD_DIM:, :] = rows[:, cols]


def block_states(chunk, group, heads, place, keys, values, step_queries):
    rows = keys.shape[0]
    steps, samples, _ = step_queries.shape
    wide = heads * HEAD_DIM
    taken = lambda m, place: (0, chunk * group + (place[0] ^ m))
    message = (heads, HEAD_DIM + steps * samples, HEAD_DIM)
    return pl.pallas_call(
        functools.partial(state_kernel, group),
        grid_spec=pltpu.PrefetchScalarGridSpec(
            num_scalar_prefetch=1,
            grid=(group,),
            in_specs=[
                pl.BlockSpec((rows, wide), taken),
                pl.BlockSpec((rows, wide), taken),
                pl.BlockSpec(
                    (steps, samples, wide), lambda m, place: (0, 0, chunk * group + (place[0] ^ m))
                ),
            ],
            out_specs=[pl.BlockSpec(message, lambda m, place: (0, 0, 0))] * group,
        ),
        out_shape=[jax.ShapeDtypeStruct(message, F32)] * group,
        compiler_params=params(("arbitrary",)),
        cost_estimate=cost(2 * rows * wide * HEAD_DIM * group, 4 * rows * wide * group),
        name="block_states",
    )(place, keys, values, step_queries)


def total_kernel(*refs):
    *parts, out_ref = refs
    total = parts[0][:, :HEAD_DIM, :]
    for part in parts[1:]:
        total = total + part[:, :HEAD_DIM, :]
    out_ref[...] = total


def group_total(parts):
    heads = parts[0].shape[0]
    shape = (heads, HEAD_DIM, HEAD_DIM)
    return pl.pallas_call(
        total_kernel,
        out_shape=jax.ShapeDtypeStruct(shape, F32),
        compiler_params=params(),
        cost_estimate=cost(0, 4 * heads * HEAD_DIM * HEAD_DIM * (len(parts) + 1)),
        name="group_total",
    )(*parts)


def prior_kernel(group, others, place_ref, *refs):
    parts, total_ref = refs[:group], refs[group]
    other_refs, out_refs = refs[group + 1 : group + 1 + others], refs[group + 1 + others :]
    place, block = place_ref[0], place_ref[1]
    heads = parts[0].shape[0]
    for h in range(heads):
        entering = jnp.zeros((HEAD_DIM, HEAD_DIM), F32)
        final = total_ref[h]
        for k in range(others):
            other = other_refs[k][h]
            entering = entering + jnp.where(block > k, other, 0.0)
            final = final + other
        high = final.astype(BF16)
        low = (final - high.astype(F32)).astype(BF16)
        for m in range(group):
            prior = entering
            for k in range(group):
                if k != m:
                    prior = prior + jnp.where(
                        (place ^ k) < (place ^ m), parts[k][h, :HEAD_DIM, :], 0.0
                    )
            out_refs[m][h, :HEAD_DIM, :] = prior
            query = parts[m][h, HEAD_DIM:, :].astype(BF16)
            out_refs[m][h, HEAD_DIM:, :] = dot(query, high) + dot(query, low)


def priors(place, parts, total, others):
    group = len(parts)
    smem = pl.BlockSpec(memory_space=pltpu.SMEM)
    vmem = pl.BlockSpec(memory_space=pltpu.VMEM)
    return pl.pallas_call(
        functools.partial(prior_kernel, group, len(others)),
        in_specs=[smem] + [vmem] * (group + 1 + len(others)),
        out_specs=[vmem] * group,
        out_shape=[jax.ShapeDtypeStruct(parts[0].shape, F32)] * group,
        compiler_params=params(),
        cost_estimate=cost(0, 4 * parts[0].size * (2 * group + 1 + len(others))),
        name="priors",
    )(place, *parts, total, *others)


def intra_kernel(tile, q_ref, k_ref, v_ref, out_ref):
    rows, wide = q_ref.shape
    keep = lax.broadcasted_iota(jnp.int32, (tile, tile), 0) >= lax.broadcasted_iota(
        jnp.int32, (tile, tile), 1
    )
    for h in range(wide // HEAD_DIM):
        cols = head_cols(h)
        for i in range(rows // tile):
            here = slice(i * tile, (i + 1) * tile)
            query = q_ref[here, cols]
            scores = dot(query, k_ref[here, cols], ((1,), (1,)))
            scores = jnp.where(keep, scores, 0.0).astype(BF16)
            total = dot(scores, v_ref[here, cols])
            if i:
                before = slice(0, i * tile)
                scores = dot(query, k_ref[before, cols], ((1,), (1,))).astype(BF16)
                total = total + dot(scores, v_ref[before, cols])
            out_ref[here, cols] = total


def intra_block(chunk, wide, queries, keys, values):
    rows = queries.shape[0]
    tile = 256 if rows % 256 == 0 else rows
    step = 2 * HEAD_DIM if wide % (2 * HEAD_DIM) == 0 else HEAD_DIM
    turns = wide // step
    spec = pl.BlockSpec((rows, step), lambda t: (0, chunk * turns + t))
    return pl.pallas_call(
        functools.partial(intra_kernel, tile),
        grid=(turns,),
        in_specs=[spec] * 3,
        out_specs=pl.BlockSpec((rows, step), lambda t: (0, t)),
        out_shape=jax.ShapeDtypeStruct((rows, wide), F32),
        compiler_params=params(("arbitrary",)),
        cost_estimate=cost(4 * rows * rows * wide, 10 * rows * wide),
        name="intra_block",
    )(queries, keys, values)


def suffix_kernel(lengths_ref, q_ref, k_ref, v_ref, sk_ref, sv_ref, out_ref):
    samples, suffix, wide = k_ref.shape
    steps = q_ref.shape[0]
    rows = steps * samples
    queries = flat_rows(q_ref).astype(BF16)
    step_keys = flat_rows(sk_ref).astype(BF16)
    step_values = flat_rows(sv_ref).astype(BF16)
    row = lax.broadcasted_iota(jnp.int32, (rows, samples * suffix), 0)
    col = lax.broadcasted_iota(jnp.int32, (rows, samples * suffix), 1)
    live = jnp.zeros((rows, samples * suffix), jnp.bool_)
    for n in range(samples):
        mine = (col >= n * suffix) & (col < n * suffix + lengths_ref[n]) & (row % samples == n)
        live = live | mine
    row = lax.broadcasted_iota(jnp.int32, (rows, rows), 0)
    col = lax.broadcasted_iota(jnp.int32, (rows, rows), 1)
    near = (row % samples == col % samples) & (row // samples >= col // samples)

    def weighted(scores, mask, values):
        scores = jnp.where(mask, scores, 0.0)
        high = scores.astype(BF16)
        low = (scores - high.astype(F32)).astype(BF16)
        return dot(high, values) + dot(low, values)

    for h in range(wide // HEAD_DIM):
        cols = head_cols(h)
        query = queries[:, cols]
        keys = k_ref[:, :, cols].reshape(samples * suffix, HEAD_DIM)
        values = v_ref[:, :, cols].reshape(samples * suffix, HEAD_DIM)
        out_ref[:, cols] = weighted(dot(query, keys, ((1,), (1,))), live, values) + weighted(
            dot(query, step_keys[:, cols], ((1,), (1,))), near, step_values[:, cols]
        )


def suffix_part(lengths, step_queries, suffix_keys, suffix_values, step_keys, step_values):
    samples, suffix, width = suffix_keys.shape
    steps = step_queries.shape[0]
    step = 2 * HEAD_DIM if width % (2 * HEAD_DIM) == 0 else HEAD_DIM
    small = pl.BlockSpec((steps, samples, step), lambda t: (0, 0, t))
    large = pl.BlockSpec((samples, suffix, step), lambda t: (0, 0, t))
    return pl.pallas_call(
        suffix_kernel,
        grid=(width // step,),
        in_specs=[pl.BlockSpec(memory_space=pltpu.SMEM), small, large, large, small, small],
        out_specs=pl.BlockSpec((steps * samples, step), lambda t: (0, t)),
        out_shape=jax.ShapeDtypeStruct((steps * samples, width), F32),
        compiler_params=params(("arbitrary",)),
        cost_estimate=cost(64 * samples * suffix * width, 4 * samples * suffix * width),
        name="suffix_part",
    )(lengths, step_queries, suffix_keys, suffix_values, step_keys, step_values)


def attended_kernel(group, first, last, place_ref, q_ref, intra_ref, extra_ref, *refs):
    parts = refs[:group]
    if first:
        before_ref, (att_ref, raw_ref, sum_ref, acc_ref) = None, refs[group:]
    else:
        before_ref, att_ref, raw_ref, sum_ref, acc_ref = refs[group:]
    rows = q_ref.shape[0]
    heads = parts[0].shape[0]
    dec = extra_ref.shape[0]
    turn = pl.program_id(0)

    @pl.when(turn == 0)
    def _():
        if first:
            acc_ref[...] = jnp.zeros_like(acc_ref)
        else:
            acc_ref[...] = before_ref[...]

    for m in range(group):

        @pl.when(turn == m)
        def _():
            squares = acc_ref[:rows, :]
            raw_squares = acc_ref[rows : rows + dec, :]
            for h in range(heads):
                cols = head_cols(h)
                prior = parts[m][h, :HEAD_DIM, :].astype(BF16)
                att = intra_ref[:, cols] + dot(q_ref[:, cols], prior)
                att_ref[:, cols] = att
                squares = squares + att * att
                raw = parts[m][h, HEAD_DIM:, :] + extra_ref[:, cols]
                raw_ref[:, cols] = raw
                raw_squares = raw_squares + raw * raw
            acc_ref[:rows, :] = squares
            acc_ref[rows : rows + dec, :] = raw_squares

    @pl.when(turn == group - 1)
    def _():
        if last:
            sum_ref[...] = jnp.sum(acc_ref[...].T, axis=0, keepdims=True)
        else:
            sum_ref[...] = acc_ref[...]


def padded_rows(rows, dec):
    return -(-(rows + dec) // LANES) * LANES


def attend(chunk, last, place, queries, intra, extra, parts, before):
    group = len(parts)
    heads = parts[0].shape[0]
    wide = heads * HEAD_DIM
    rows, dec = queries.shape[0], extra.shape[0]
    padded = padded_rows(rows, dec)
    whole = lambda m, place: (0, chunk * group + (place[0] ^ m))
    own = lambda m, place: (0, place[0] ^ m)
    fixed = lambda m, place: (0, 0)
    sums = (1, padded) if last else (padded, LANES)
    first = before is None
    return pl.pallas_call(
        functools.partial(attended_kernel, group, first, last),
        grid_spec=pltpu.PrefetchScalarGridSpec(
            num_scalar_prefetch=1,
            grid=(group,),
            in_specs=[
                pl.BlockSpec((rows, wide), whole),
                pl.BlockSpec((rows, wide), own),
                pl.BlockSpec((dec, wide), whole),
            ]
            + [pl.BlockSpec(parts[0].shape, lambda m, place: (0, 0, 0))] * group
            + ([] if first else [pl.BlockSpec((padded, LANES), fixed)]),
            out_specs=[
                pl.BlockSpec((rows, wide), own),
                pl.BlockSpec((dec, wide), own),
                pl.BlockSpec(sums, fixed),
            ],
            scratch_shapes=[pltpu.VMEM((padded, LANES), F32)],
        ),
        out_shape=[
            jax.ShapeDtypeStruct((rows, wide * group), F32),
            jax.ShapeDtypeStruct((dec, wide * group), F32),
            jax.ShapeDtypeStruct(sums, F32),
        ],
        compiler_params=params(("arbitrary",)),
        cost_estimate=cost(2 * rows * wide * group * HEAD_DIM, 10 * rows * wide * group),
        name="attend",
    )(place, queries, intra, extra, *parts, *([] if first else [before]))


def norm_kernel(chunks, sums, width, gain_ref, *refs):
    sum_refs = refs[:sums]
    att_refs = refs[sums : sums + chunks]
    raw_refs = refs[sums + chunks : sums + 2 * chunks]
    out_ref, dec_ref, scale_ref = refs[sums + 2 * chunks :]
    tile = out_ref.shape[0]
    dec = raw_refs[0].shape[0]
    rows = tile * pl.num_programs(0)
    turn = pl.program_id(0)
    wide = att_refs[0].shape[1]

    @pl.when(turn == 0)
    def _():
        total = sum_refs[0][...]
        for ref in sum_refs[1:]:
            total = total + ref[...]
        scale = lax.rsqrt(total / width + 1e-06)
        scale_ref[...] = jnp.broadcast_to(scale, (LANES, scale.shape[1])).T
        samples = dec_ref.shape[1]
        here = scale_ref[pl.ds(tile * pl.num_programs(0), dec), :]
        for c in range(chunks):
            for h in range(wide // HEAD_DIM):
                cols = head_cols(h)
                at = slice(c * wide + h * HEAD_DIM, c * wide + (h + 1) * HEAD_DIM)
                out = raw_refs[c][:, cols] * here * gain_ref[:, at]
                for i in range(dec_ref.shape[0]):
                    dec_ref[i, :, at] = out[i * samples : (i + 1) * samples].astype(BF16)

    here = scale_ref[pl.ds(pl.multiple_of(turn * tile, tile), tile), :]
    for c in range(chunks):
        for h in range(wide // HEAD_DIM):
            cols = head_cols(h)
            at = slice(c * wide + h * HEAD_DIM, c * wide + (h + 1) * HEAD_DIM)
            out_ref[:, at] = (att_refs[c][:, cols] * here * gain_ref[:, at]).astype(BF16)


def normalize(atts, raws, sums, gain, steps, width_all):
    rows, wide = atts[0].shape
    width = wide * len(atts)
    dec = raws[0].shape[0]
    tile = 128 if rows % 128 == 0 else rows
    fixed = lambda t: (0, 0)
    return pl.pallas_call(
        functools.partial(norm_kernel, len(atts), len(sums), width_all),
        grid=(rows // tile,),
        in_specs=[pl.BlockSpec((1, width), fixed)]
        + [pl.BlockSpec(sums[0].shape, fixed)] * len(sums)
        + [pl.BlockSpec((tile, wide), lambda t: (t, 0))] * len(atts)
        + [pl.BlockSpec((dec, wide), fixed)] * len(raws),
        out_specs=[
            pl.BlockSpec((tile, width), lambda t: (t, 0)),
            pl.BlockSpec((steps, dec // steps, width), lambda t: (0, 0, 0)),
        ],
        out_shape=[
            jax.ShapeDtypeStruct((rows, width), BF16),
            jax.ShapeDtypeStruct((steps, dec // steps, width), BF16),
        ],
        scratch_shapes=[pltpu.VMEM((sums[0].shape[1], LANES), F32)],
        compiler_params=params(("arbitrary",)),
        cost_estimate=cost(0, 6 * rows * width),
        name="normalize",
    )(gain[None, :], *sums, *atts, *raws)


def group_size(devices, heads):
    size = 1
    while (
        devices % (2 * size) == 0
        and size * size < devices
        and heads % (2 * size * CHUNKS) == 0
    ):
        size *= 2
    return size


def on_device(
    queries,
    keys,
    values,
    suffix_keys,
    suffix_values,
    suffix_lengths,
    step_queries,
    step_keys,
    step_values,
    norm_gain,
):
    width = queries.shape[1]
    heads_here = width // HEAD_DIM
    devices = lax.axis_size("seq")
    group = group_size(devices, heads_here)
    blocks = devices // group
    heads = heads_here // (group * CHUNKS)
    rank = lax.axis_index("seq")
    place = jnp.stack([rank % group, rank // group]).astype(jnp.int32)

    def swap(m):
        return [(i, i // group * group + (i % group ^ m)) for i in range(devices)]

    def exchange(messages):
        return [messages[0]] + [
            lax.ppermute(messages[m], "seq", swap(m)) for m in range(1, group)
        ]

    chunks = range(CHUNKS)
    parts = [
        exchange(block_states(c, group, heads, place, keys, values, step_queries)) for c in chunks
    ]
    totals = [group_total(parts[c]) for c in chunks]
    others = [
        [
            lax.ppermute(
                totals[c], "seq", [(i, (i + k * group) % devices) for i in range(devices)]
            )
            for k in range(1, blocks)
        ]
        for c in chunks
    ]
    entering = [exchange(priors(place, parts[c], totals[c], others[c])) for c in chunks]
    intra = [intra_block(c, width // CHUNKS, queries, keys, values) for c in chunks]
    extra = suffix_part(
        suffix_lengths, step_queries, suffix_keys, suffix_values, step_keys, step_values
    )
    atts, raws, sums = [], [], None
    for c in chunks:
        att, raw, sums = attend(
            c, c == CHUNKS - 1, place, queries, intra[c], extra, entering[c], sums
        )
        atts.append(att)
        raws.append(raw)
    others_of_row = lax.axis_size("head")
    all_sums = [sums] + [
        lax.ppermute(
            sums, "head", [(i, (i + k) % others_of_row) for i in range(others_of_row)]
        )
        for k in range(1, others_of_row)
    ]
    return tuple(
        normalize(
            atts, raws, all_sums, norm_gain, step_queries.shape[0], width * others_of_row
        )
    )


def solution(mesh):
    return jax.shard_map(
        on_device,
        mesh=mesh,
        in_specs=(
            P("seq", "head"),
            P("seq", "head"),
            P("seq", "head"),
            P("seq", None, "head"),
            P("seq", None, "head"),
            P("seq"),
            P(None, "seq", "head"),
            P(None, "seq", "head"),
            P(None, "seq", "head"),
            P("head"),
        ),
        out_specs=(P("seq", "head"), P(None, "seq", "head")),
        check_vma=False,
    )
```

```python
import functools

import jax
import jax.numpy as jnp
from jax import lax
from jax.experimental import pallas as pl
from jax.experimental.pallas import tpu as pltpu
from jax.sharding import PartitionSpec as P

HEAD_DIM = 128
LANES = 128
CHUNKS = 2
F32 = jnp.float32
BF16 = jnp.bfloat16
VMEM_LIMIT = 24 * 1024 * 1024
SMEM = pl.BlockSpec(memory_space=pltpu.SMEM)
VMEM = pl.BlockSpec(memory_space=pltpu.VMEM)
ANY = pl.BlockSpec(memory_space=pl.ANY)


def dot(a, b, contract=((1,), (0,))):
    return lax.dot_general(a, b, (contract, ((), ())), preferred_element_type=F32)


def params():
    return pltpu.CompilerParams(vmem_limit_bytes=VMEM_LIMIT)


def cost(flops, moved):
    return pl.CostEstimate(flops=int(flops), bytes_accessed=int(moved), transcendentals=0)


def head_cols(head):
    return slice(head * HEAD_DIM, (head + 1) * HEAD_DIM)


def flat_rows(ref):
    return jnp.concatenate([ref[i].astype(F32) for i in range(ref.shape[0])], axis=0)


def owned_cols(place_ref, m, first, heads):
    wide = heads * HEAD_DIM
    return pl.ds(pl.multiple_of(first + (place_ref[0] ^ m) * wide, wide), wide)


def split(x):
    high = x.astype(BF16)
    return high, (x - high.astype(F32)).astype(BF16)


def state_kernel(group, first, place_ref, q_ref, k_hbm, v_hbm, *refs):
    out_refs, (k_buf, v_buf, sems) = refs[:group], refs[group:]
    heads = out_refs[0].shape[0]
    order = [*range(1, group), 0]
    copies = {}
    for m in order:
        cols = owned_cols(place_ref, m, first, heads)
        copies[m] = [
            pltpu.make_async_copy(k_hbm.at[:, cols], k_buf.at[m], sems.at[m, 0]),
            pltpu.make_async_copy(v_hbm.at[:, cols], v_buf.at[m], sems.at[m, 1]),
        ]
        for copy in copies[m]:
            copy.start()
    for m in order:
        rows = jnp.concatenate(
            [
                q_ref[i, :, owned_cols(place_ref, m, first, heads)].astype(F32)
                for i in range(q_ref.shape[0])
            ],
            axis=0,
        )
        for copy in copies[m]:
            copy.wait()
        for h in range(heads):
            cols = head_cols(h)
            out_refs[m][h, :HEAD_DIM, :] = dot(k_buf[m, :, cols], v_buf[m, :, cols], ((0,), (0,)))
            out_refs[m][h, HEAD_DIM:, :] = rows[:, cols]


def block_states(chunk, group, heads, place, keys, values, step_queries):
    rows = keys.shape[0]
    steps, samples, _ = step_queries.shape
    wide = heads * HEAD_DIM
    message = (heads, HEAD_DIM + steps * samples, HEAD_DIM)
    hbm = pl.BlockSpec(memory_space=pltpu.HBM)
    return pl.pallas_call(
        functools.partial(state_kernel, group, chunk * group * wide),
        in_specs=[SMEM, VMEM, hbm, hbm],
        out_specs=[VMEM] * group,
        out_shape=[jax.ShapeDtypeStruct(message, F32)] * group,
        scratch_shapes=[
            pltpu.VMEM((group, rows, wide), keys.dtype),
            pltpu.VMEM((group, rows, wide), values.dtype),
            pltpu.SemaphoreType.DMA((group, 2)),
        ],
        compiler_params=params(),
        cost_estimate=cost(2 * rows * wide * HEAD_DIM * group, 4 * rows * wide * group),
        name="block_states",
    )(
        place,
        step_queries,
        pltpu.with_memory_space_constraint(keys, pltpu.HBM),
        pltpu.with_memory_space_constraint(values, pltpu.HBM),
    )


def total_kernel(group, *refs):
    total = refs[0][:, :HEAD_DIM, :]
    for part in refs[1:group]:
        total = total + part[:, :HEAD_DIM, :]
    refs[-1][...] = total


def group_total(parts, after):
    heads = parts[0].shape[0]
    shape = (heads, HEAD_DIM, HEAD_DIM)
    return pl.pallas_call(
        functools.partial(total_kernel, len(parts)),
        in_specs=[VMEM] * len(parts) + [ANY] * len(after),
        out_specs=VMEM,
        out_shape=jax.ShapeDtypeStruct(shape, F32),
        compiler_params=params(),
        cost_estimate=cost(0, 4 * heads * HEAD_DIM * HEAD_DIM * (len(parts) + 1)),
        name="group_total",
    )(*parts, *after)


def prior_kernel(group, others, place_ref, *refs):
    parts, total_ref = refs[:group], refs[group]
    other_refs, out_refs = refs[group + 1 : group + 1 + others], refs[-group:]
    place, block = place_ref[0], place_ref[1]
    heads = parts[0].shape[0]
    for h in range(heads):
        entering = jnp.zeros((HEAD_DIM, HEAD_DIM), F32)
        final = total_ref[h]
        for k in range(others):
            other = other_refs[k][h]
            entering = entering + jnp.where(block > k, other, 0.0)
            final = final + other
        high, low = split(final)
        query = jnp.concatenate([part[h, HEAD_DIM:, :] for part in parts], axis=0).astype(BF16)
        raw = dot(query, high) + dot(query, low)
        dec = raw.shape[0] // group
        for m in range(group):
            prior = entering
            for k in range(group):
                if k != m:
                    prior = prior + jnp.where(
                        (place ^ k) < (place ^ m), parts[k][h, :HEAD_DIM, :], 0.0
                    )
            out_refs[m][h, :HEAD_DIM, :] = prior
            out_refs[m][h, HEAD_DIM:, :] = raw[m * dec : (m + 1) * dec]


def priors(place, parts, total, others, after):
    group = len(parts)
    return pl.pallas_call(
        functools.partial(prior_kernel, group, len(others)),
        in_specs=[SMEM] + [VMEM] * (group + 1 + len(others)) + [ANY] * len(after),
        out_specs=[VMEM] * group,
        out_shape=[jax.ShapeDtypeStruct(parts[0].shape, F32)] * group,
        compiler_params=params(),
        cost_estimate=cost(0, 4 * parts[0].size * (2 * group + 1 + len(others))),
        name="priors",
    )(place, *parts, total, *others, *after)


def intra_kernel(tile, first, q_ref, k_ref, v_ref, *refs):
    out_ref = refs[-1]
    rows, wide = out_ref.shape
    keep = lax.broadcasted_iota(jnp.int32, (tile, tile), 0) >= lax.broadcasted_iota(
        jnp.int32, (tile, tile), 1
    )
    for h in range(wide // HEAD_DIM):
        cols = slice(first + h * HEAD_DIM, first + (h + 1) * HEAD_DIM)
        for i in range(rows // tile):
            here = slice(i * tile, (i + 1) * tile)
            query = q_ref[here, cols]
            scores = dot(query, k_ref[here, cols], ((1,), (1,)))
            scores = jnp.where(keep, scores, 0.0).astype(BF16)
            total = dot(scores, v_ref[here, cols])
            if i:
                before = slice(0, i * tile)
                scores = dot(query, k_ref[before, cols], ((1,), (1,))).astype(BF16)
                total = total + dot(scores, v_ref[before, cols])
            out_ref[here, head_cols(h)] = total


def intra_block(first, wide, queries, keys, values, after):
    rows = queries.shape[0]
    tile = 256 if rows % 256 == 0 else rows
    return pl.pallas_call(
        functools.partial(intra_kernel, tile, first),
        in_specs=[VMEM] * 3 + [ANY] * len(after),
        out_specs=VMEM,
        out_shape=jax.ShapeDtypeStruct((rows, wide), F32),
        compiler_params=params(),
        cost_estimate=cost(4 * rows * rows * wide, 10 * rows * wide),
        name="intra_block",
    )(queries, keys, values, *after)


def suffix_kernel(lengths_ref, q_ref, k_ref, v_ref, sk_ref, sv_ref, *refs):
    out_ref = refs[-1]
    samples, suffix, width = k_ref.shape
    steps = q_ref.shape[0]
    rows = steps * samples
    tokens = samples * suffix
    heads = max(1, min(LANES // rows, width // HEAD_DIM))
    queries = flat_rows(q_ref)
    step_keys = flat_rows(sk_ref).astype(BF16)
    step_values = flat_rows(sv_ref).astype(BF16)

    at = lax.broadcasted_iota(jnp.int32, (heads * rows, tokens), 0) % samples
    token = lax.broadcasted_iota(jnp.int32, (heads * rows, tokens), 1)
    ends = jnp.zeros((heads * rows, tokens), jnp.int32)
    for n in range(samples):
        ends = jnp.where(at == n, n * suffix + lengths_ref[n], ends)
    live = (token >= at * suffix) & (token < ends)
    row = lax.broadcasted_iota(jnp.int32, (heads * rows, rows), 0) % rows
    col = lax.broadcasted_iota(jnp.int32, (heads * rows, rows), 1)
    near = (row % samples == col % samples) & (row // samples >= col // samples)

    for top in range(0, width // HEAD_DIM, heads):
        scores = jnp.zeros((tokens, heads * rows), F32)
        step_scores = jnp.zeros((rows, heads * rows), F32)
        for h in range(heads):
            cols = head_cols(top + h)
            query = queries[:, cols]
            pieces = [jnp.zeros((h * rows, HEAD_DIM), F32)] if h else []
            pieces.append(query)
            if h < heads - 1:
                pieces.append(jnp.zeros(((heads - 1 - h) * rows, HEAD_DIM), F32))
            placed = jnp.concatenate(pieces, axis=0).astype(BF16)
            keys = k_ref[:, :, cols].reshape(tokens, HEAD_DIM)
            scores = scores + dot(keys, placed, ((1,), (1,)))
            step_scores = step_scores + dot(step_keys[:, cols], placed, ((1,), (1,)))
        high, low = split(jnp.where(live, scores.T, 0.0))
        step_high, step_low = split(jnp.where(near, step_scores.T, 0.0))
        for h in range(heads):
            cols = head_cols(top + h)
            own = slice(h * rows, (h + 1) * rows)
            values = v_ref[:, :, cols].reshape(tokens, HEAD_DIM)
            out_ref[:, cols] = (
                dot(high[own], values)
                + dot(low[own], values)
                + dot(step_high[own], step_values[:, cols])
                + dot(step_low[own], step_values[:, cols])
            )


def suffix_part(lengths, step_queries, suffix_keys, suffix_values, step_keys, step_values, after):
    samples, suffix, width = suffix_keys.shape
    steps = step_queries.shape[0]
    return pl.pallas_call(
        suffix_kernel,
        in_specs=[SMEM] + [VMEM] * 5 + [ANY] * len(after),
        out_specs=VMEM,
        out_shape=jax.ShapeDtypeStruct((steps * samples, width), F32),
        compiler_params=params(),
        cost_estimate=cost(64 * samples * suffix * width, 4 * samples * suffix * width),
        name="suffix_part",
    )(lengths, step_queries, suffix_keys, suffix_values, step_keys, step_values, *after)


def attended_kernel(group, top, first, last, place_ref, q_ref, intra_ref, extra_ref, *refs):
    parts = refs[:group]
    att_ref, raw_ref, sum_ref, acc_ref = refs[-4:]
    rows = q_ref.shape[0]
    heads = parts[0].shape[0]
    dec = extra_ref.shape[0]
    if first:
        acc_ref[...] = jnp.zeros_like(acc_ref)
    else:
        acc_ref[...] = refs[group][...]
    for m in range(group):
        all_cols = owned_cols(place_ref, m, top, heads)
        own_cols = owned_cols(place_ref, m, 0, heads)
        query = q_ref[:, all_cols]
        intra = intra_ref[:, own_cols]
        extra = extra_ref[:, all_cols]
        squares = acc_ref[:rows, :]
        raw_squares = acc_ref[rows : rows + dec, :]
        atts, raws = [], []
        for h in range(heads):
            cols = head_cols(h)
            att = intra[:, cols] + dot(query[:, cols], parts[m][h, :HEAD_DIM, :].astype(BF16))
            raw = extra[:, cols] + parts[m][h, HEAD_DIM:, :]
            squares = squares + att * att
            raw_squares = raw_squares + raw * raw
            atts.append(att)
            raws.append(raw)
        att_ref[:, own_cols] = jnp.concatenate(atts, axis=1)
        raw_ref[:, own_cols] = jnp.concatenate(raws, axis=1)
        acc_ref[:rows, :] = squares
        acc_ref[rows : rows + dec, :] = raw_squares
    if last:
        sum_ref[...] = jnp.sum(acc_ref[...].T, axis=0, keepdims=True)
    else:
        sum_ref[...] = acc_ref[...]


def attend(chunk, last, place, queries, intra, extra, parts, before, after):
    group = len(parts)
    heads = parts[0].shape[0]
    wide = group * heads * HEAD_DIM
    rows, dec = queries.shape[0], extra.shape[0]
    padded = -(-(rows + dec) // LANES) * LANES
    sums = (1, padded) if last else (padded, LANES)
    return pl.pallas_call(
        functools.partial(attended_kernel, group, chunk * wide, not before, last),
        in_specs=[SMEM] + [VMEM] * (3 + group + len(before)) + [ANY] * len(after),
        out_specs=[VMEM] * 3,
        out_shape=[
            jax.ShapeDtypeStruct((rows, wide), F32),
            jax.ShapeDtypeStruct((dec, wide), F32),
            jax.ShapeDtypeStruct(sums, F32),
        ],
        scratch_shapes=[pltpu.VMEM((padded, LANES), F32)],
        compiler_params=params(),
        cost_estimate=cost(2 * rows * wide * HEAD_DIM, 10 * rows * wide),
        name="attend",
    )(place, queries, intra, extra, *parts, *before, *after)


def norm_kernel(chunks, sums, width, tile, gain_ref, *refs):
    sum_refs = refs[:sums]
    att_refs = refs[sums : sums + chunks]
    raw_refs = refs[sums + chunks : sums + 2 * chunks]
    out_hbm, dec_ref, scale_ref, buf_ref, sems = refs[sums + 2 * chunks :]
    rows, wide = att_refs[0].shape
    dec = raw_refs[0].shape[0]
    samples = dec_ref.shape[1]
    total = sum_refs[0][...]
    for ref in sum_refs[1:]:
        total = total + ref[...]
    scale = lax.rsqrt(total / width + 1e-06)
    scale_ref[...] = jnp.broadcast_to(scale, (LANES, scale.shape[1])).T
    copies = []
    for i in range(rows // tile):
        here = slice(i * tile, (i + 1) * tile)
        row_scale = scale_ref[here, :]
        for c in range(chunks):
            for h in range(wide // HEAD_DIM):
                at = slice(c * wide + h * HEAD_DIM, c * wide + (h + 1) * HEAD_DIM)
                buf_ref[here, at] = (
                    att_refs[c][here, head_cols(h)] * row_scale * gain_ref[:, at]
                ).astype(BF16)
        copies.append(pltpu.make_async_copy(buf_ref.at[here], out_hbm.at[here], sems.at[i]))
        copies[-1].start()
    row_scale = scale_ref[rows : rows + dec, :]
    for c in range(chunks):
        for h in range(wide // HEAD_DIM):
            at = slice(c * wide + h * HEAD_DIM, c * wide + (h + 1) * HEAD_DIM)
            out = raw_refs[c][:, head_cols(h)] * row_scale * gain_ref[:, at]
            for i in range(dec_ref.shape[0]):
                dec_ref[i, :, at] = out[i * samples : (i + 1) * samples].astype(BF16)
    for copy in copies:
        copy.wait()


def normalize(atts, raws, sums, gain, steps, width_all):
    rows, wide = atts[0].shape
    width = wide * len(atts)
    dec = raws[0].shape[0]
    tile = 128 if rows % 128 == 0 else rows
    return pl.pallas_call(
        functools.partial(norm_kernel, len(atts), len(sums), width_all, tile),
        in_specs=[VMEM] * (1 + len(sums) + 2 * len(atts)),
        out_specs=[pl.BlockSpec(memory_space=pltpu.HBM), VMEM],
        out_shape=[
            jax.ShapeDtypeStruct((rows, width), BF16),
            jax.ShapeDtypeStruct((steps, dec // steps, width), BF16),
        ],
        scratch_shapes=[
            pltpu.VMEM((sums[0].shape[1], LANES), F32),
            pltpu.VMEM((rows, width), BF16),
            pltpu.SemaphoreType.DMA((rows // tile,)),
        ],
        compiler_params=params(),
        cost_estimate=cost(0, 6 * rows * width),
        name="normalize",
    )(gain[None, :], *sums, *atts, *raws)


def group_size(devices, heads):
    size = 1
    while (
        devices % (2 * size) == 0
        and size * size < devices
        and heads % (2 * size * CHUNKS) == 0
    ):
        size *= 2
    return size


def on_device(
    queries,
    keys,
    values,
    suffix_keys,
    suffix_values,
    suffix_lengths,
    step_queries,
    step_keys,
    step_values,
    norm_gain,
):
    width = queries.shape[1]
    heads_here = width // HEAD_DIM
    devices = lax.axis_size("seq")
    group = group_size(devices, heads_here)
    blocks = devices // group
    heads = heads_here // (group * CHUNKS)
    rank = lax.axis_index("seq")
    place = jnp.stack([rank % group, rank // group]).astype(jnp.int32)

    def swap(m):
        return [(i, i // group * group + (i % group ^ m)) for i in range(devices)]

    def exchange(messages):
        return [messages[0]] + [
            lax.ppermute(messages[m], "seq", swap(m)) for m in range(1, group)
        ]

    def across(total):
        return [
            lax.ppermute(total, "seq", [(i, (i + k * group) % devices) for i in range(devices)])
            for k in range(1, blocks)
        ]

    wide = width // CHUNKS
    parts, totals, others, entering, intra = [], [], [], [], []
    for c in range(CHUNKS):
        parts.append(exchange(block_states(c, group, heads, place, keys, values, step_queries)))
    last = [parts[-1][0]]
    for c in range(CHUNKS):
        if c == 0 or CHUNKS == 1:
            last = [intra_block(c * wide, wide, queries, keys, values, last)]
            intra += last
        totals.append(group_total(parts[c], last))
        others.append(across(totals[c]))
        if c == 0 and CHUNKS > 1:
            last = [intra_block(wide, width - wide, queries, keys, values, [totals[c]])]
            intra += last
        else:
            extra = suffix_part(
                suffix_lengths,
                step_queries,
                suffix_keys,
                suffix_values,
                step_keys,
                step_values,
                [totals[c]],
            )
            last = [extra]
        sent = priors(place, parts[c], totals[c], others[c], last)
        entering.append(exchange(sent))
        last = [sent[0]]
    atts, raws, sums = [], [], []
    for c in range(CHUNKS):
        att, raw, total = attend(
            c, c == CHUNKS - 1, place, queries, intra[c], extra, entering[c], sums, last
        )
        sums = [total]
        atts.append(att)
        raws.append(raw)
    sums = sums[0]
    others_of_row = lax.axis_size("head")
    all_sums = [sums] + [
        lax.ppermute(
            sums, "head", [(i, (i + k) % others_of_row) for i in range(others_of_row)]
        )
        for k in range(1, others_of_row)
    ]
    return tuple(
        normalize(
            atts, raws, all_sums, norm_gain, step_queries.shape[0], width * others_of_row
        )
    )


def solution(mesh):
    return jax.shard_map(
        on_device,
        mesh=mesh,
        in_specs=(
            P("seq", "head"),
            P("seq", "head"),
            P("seq", "head"),
            P("seq", None, "head"),
            P("seq", None, "head"),
            P("seq"),
            P(None, "seq", "head"),
            P(None, "seq", "head"),
            P(None, "seq", "head"),
            P("head"),
        ),
        out_specs=(P("seq", "head"), P(None, "seq", "head")),
        check_vma=False,
    )
```

```python
import functools

import jax
import jax.numpy as jnp
from jax import lax
from jax.experimental import pallas as pl
from jax.experimental.pallas import tpu as pltpu
from jax.sharding import PartitionSpec as P

HEAD_DIM = 128
LANES = 128
CHUNKS = 2
F32 = jnp.float32
BF16 = jnp.bfloat16
VMEM_LIMIT = 24 * 1024 * 1024
SMEM = pl.BlockSpec(memory_space=pltpu.SMEM)
VMEM = pl.BlockSpec(memory_space=pltpu.VMEM)
ANY = pl.BlockSpec(memory_space=pl.ANY)


def dot(a, b, contract=((1,), (0,))):
    return lax.dot_general(a, b, (contract, ((), ())), preferred_element_type=F32)


def params():
    return pltpu.CompilerParams(vmem_limit_bytes=VMEM_LIMIT)


def cost(flops, moved):
    return pl.CostEstimate(flops=int(flops), bytes_accessed=int(moved), transcendentals=0)


def head_cols(head):
    return slice(head * HEAD_DIM, (head + 1) * HEAD_DIM)


def flat_rows(ref):
    return jnp.concatenate([ref[i].astype(F32) for i in range(ref.shape[0])], axis=0)


def place(group):
    rank = lax.axis_index("seq")
    return lax.rem(rank, group), lax.div(rank, group)


def owned_cols(group, m, first, heads):
    wide = heads * HEAD_DIM
    return pl.ds(pl.multiple_of(first + (place(group)[0] ^ m) * wide, wide), wide)


def split(x):
    high = x.astype(BF16)
    return high, (x - high.astype(F32)).astype(BF16)


def message(out_ref, rows, keys, values):
    for h in range(out_ref.shape[0]):
        cols = head_cols(h)
        out_ref[h, :HEAD_DIM, :] = dot(keys[:, cols], values[:, cols], ((0,), (0,)))
        out_ref[h, HEAD_DIM:, :] = rows[:, cols]


def step_rows(q_ref, cols):
    return jnp.concatenate([q_ref[i, :, cols].astype(F32) for i in range(q_ref.shape[0])], axis=0)


def fetched_state_kernel(group, m, first, q_hbm, k_hbm, v_hbm, out_ref, q_buf, k_buf, v_buf, sems):
    cols = owned_cols(group, m, first, out_ref.shape[0])
    copies = [
        pltpu.make_async_copy(k_hbm.at[:, cols], k_buf, sems.at[0]),
        pltpu.make_async_copy(v_hbm.at[:, cols], v_buf, sems.at[1]),
        pltpu.make_async_copy(q_hbm.at[:, :, cols], q_buf, sems.at[2]),
    ]
    for copy in copies:
        copy.start()
    for copy in copies:
        copy.wait()
    message(out_ref, step_rows(q_buf, slice(None)), k_buf[...], v_buf[...])


def fetched_states(m, chunk, group, heads, keys, values, step_queries):
    rows = keys.shape[0]
    steps, samples, _ = step_queries.shape
    wide = heads * HEAD_DIM
    hbm = pl.BlockSpec(memory_space=pltpu.HBM)
    return pl.pallas_call(
        functools.partial(fetched_state_kernel, group, m, chunk * group * wide),
        in_specs=[hbm, hbm, hbm],
        out_specs=VMEM,
        out_shape=jax.ShapeDtypeStruct((heads, HEAD_DIM + steps * samples, HEAD_DIM), F32),
        scratch_shapes=[
            pltpu.VMEM((steps, samples, wide), step_queries.dtype),
            pltpu.VMEM((rows, wide), keys.dtype),
            pltpu.VMEM((rows, wide), values.dtype),
            pltpu.SemaphoreType.DMA((3,)),
        ],
        compiler_params=params(),
        cost_estimate=cost(2 * rows * wide * HEAD_DIM, 4 * rows * wide),
        name="fetched_states",
    )(
        pltpu.with_memory_space_constraint(step_queries, pltpu.HBM),
        pltpu.with_memory_space_constraint(keys, pltpu.HBM),
        pltpu.with_memory_space_constraint(values, pltpu.HBM),
    )


def state_kernel(group, owners, first, q_ref, k_ref, v_ref, *refs):
    out_refs = refs[-len(owners) :]
    for m, out_ref in zip(owners, out_refs):
        cols = owned_cols(group, m, first, out_ref.shape[0])
        message(out_ref, step_rows(q_ref, cols), k_ref[:, cols], v_ref[:, cols])


def block_states(owners, chunk, group, heads, keys, values, step_queries, after):
    rows = keys.shape[0]
    steps, samples, _ = step_queries.shape
    wide = heads * HEAD_DIM
    shape = jax.ShapeDtypeStruct((heads, HEAD_DIM + steps * samples, HEAD_DIM), F32)
    return pl.pallas_call(
        functools.partial(state_kernel, group, owners, chunk * group * wide),
        in_specs=[VMEM, VMEM, VMEM] + [ANY] * len(after),
        out_specs=[VMEM] * len(owners),
        out_shape=[shape] * len(owners),
        compiler_params=params(),
        cost_estimate=cost(2 * rows * wide * HEAD_DIM * len(owners), 4 * rows * wide * len(owners)),
        name="block_states",
    )(step_queries, keys, values, *after)


def total_kernel(group, *refs):
    total = refs[0][:, :HEAD_DIM, :]
    for part in refs[1:group]:
        total = total + part[:, :HEAD_DIM, :]
    refs[-1][...] = total


def group_total(parts, after):
    heads = parts[0].shape[0]
    shape = (heads, HEAD_DIM, HEAD_DIM)
    return pl.pallas_call(
        functools.partial(total_kernel, len(parts)),
        in_specs=[VMEM] * len(parts) + [ANY] * len(after),
        out_specs=VMEM,
        out_shape=jax.ShapeDtypeStruct(shape, F32),
        compiler_params=params(),
        cost_estimate=cost(0, 4 * heads * HEAD_DIM * HEAD_DIM * (len(parts) + 1)),
        name="group_total",
    )(*parts, *after)


def prior_kernel(group, others, *refs):
    parts, total_ref = refs[:group], refs[group]
    other_refs, out_refs = refs[group + 1 : group + 1 + others], refs[-group:]
    here, block = place(group)
    heads = parts[0].shape[0]
    for h in range(heads):
        entering = jnp.zeros((HEAD_DIM, HEAD_DIM), F32)
        final = total_ref[h]
        for k in range(others):
            other = other_refs[k][h]
            entering = entering + jnp.where(block > k, other, 0.0)
            final = final + other
        high, low = split(final)
        query = jnp.concatenate([part[h, HEAD_DIM:, :] for part in parts], axis=0).astype(BF16)
        raw = dot(query, high) + dot(query, low)
        dec = raw.shape[0] // group
        for m in range(group):
            prior = entering
            for k in range(group):
                if k != m:
                    prior = prior + jnp.where(
                        (here ^ k) < (here ^ m), parts[k][h, :HEAD_DIM, :], 0.0
                    )
            out_refs[m][h, :HEAD_DIM, :] = prior
            out_refs[m][h, HEAD_DIM:, :] = raw[m * dec : (m + 1) * dec]


def priors(parts, total, others, after):
    group = len(parts)
    return pl.pallas_call(
        functools.partial(prior_kernel, group, len(others)),
        in_specs=[VMEM] * (group + 1 + len(others)) + [ANY] * len(after),
        out_specs=[VMEM] * group,
        out_shape=[jax.ShapeDtypeStruct(parts[0].shape, F32)] * group,
        compiler_params=params(),
        cost_estimate=cost(0, 4 * parts[0].size * (2 * group + 1 + len(others))),
        name="priors",
    )(*parts, total, *others, *after)


def intra_kernel(tile, first, q_ref, k_ref, v_ref, *refs):
    out_ref = refs[-1]
    rows, wide = out_ref.shape
    keep = lax.broadcasted_iota(jnp.int32, (tile, tile), 0) >= lax.broadcasted_iota(
        jnp.int32, (tile, tile), 1
    )
    for h in range(wide // HEAD_DIM):
        cols = slice(first + h * HEAD_DIM, first + (h + 1) * HEAD_DIM)
        total = None
        for i in range(0, rows, tile):
            scores = dot(q_ref[i:, cols], k_ref[i : i + tile, cols], ((1,), (1,)))
            near = jnp.where(keep, scores[:tile], 0.0).astype(BF16)
            if i + tile < rows:
                near = jnp.concatenate([near, scores[tile:].astype(BF16)], axis=0)
            part = dot(near, v_ref[i : i + tile, cols])
            total = part if total is None else total + part
            out_ref[i : i + tile, head_cols(h)] = total[:tile]
            total = total[tile:]


def intra_block(first, wide, queries, keys, values, after):
    rows = queries.shape[0]
    tile = 256 if rows % 256 == 0 else rows
    return pl.pallas_call(
        functools.partial(intra_kernel, tile, first),
        in_specs=[VMEM] * 3 + [ANY] * len(after),
        out_specs=VMEM,
        out_shape=jax.ShapeDtypeStruct((rows, wide), F32),
        compiler_params=params(),
        cost_estimate=cost(4 * rows * rows * wide, 10 * rows * wide),
        name="intra_block",
    )(queries, keys, values, *after)


def suffix_kernel(lengths_ref, q_ref, k_ref, v_ref, sk_ref, sv_ref, *refs):
    out_ref = refs[-1]
    samples, suffix, width = k_ref.shape
    steps = q_ref.shape[0]
    rows = steps * samples
    tokens = samples * suffix
    heads = max(1, min(LANES // rows, width // HEAD_DIM))
    queries = flat_rows(q_ref)
    step_keys = flat_rows(sk_ref).astype(BF16)
    step_values = flat_rows(sv_ref).astype(BF16)

    at = lax.broadcasted_iota(jnp.int32, (heads * rows, tokens), 0) % samples
    token = lax.broadcasted_iota(jnp.int32, (heads * rows, tokens), 1)
    ends = jnp.zeros((heads * rows, tokens), jnp.int32)
    for n in range(samples):
        ends = jnp.where(at == n, n * suffix + lengths_ref[n], ends)
    live = (token >= at * suffix) & (token < ends)
    row = lax.broadcasted_iota(jnp.int32, (heads * rows, rows), 0) % rows
    col = lax.broadcasted_iota(jnp.int32, (heads * rows, rows), 1)
    near = (row % samples == col % samples) & (row // samples >= col // samples)

    pair = 2 if heads % 2 == 0 else 1
    wide = pair * HEAD_DIM
    for top in range(0, width // HEAD_DIM, heads):
        scores = jnp.zeros((tokens, heads * rows), F32)
        step_scores = jnp.zeros((rows, heads * rows), F32)
        for h in range(0, heads, pair):
            cols = slice((top + h) * HEAD_DIM, (top + h) * HEAD_DIM + wide)
            pieces = []
            for p in range(pair):
                own = [jnp.zeros((rows, HEAD_DIM), F32)] * pair
                own[p] = queries[:, head_cols(top + h + p)]
                pieces.append(jnp.concatenate(own, axis=1))
            if h:
                pieces.insert(0, jnp.zeros((h * rows, wide), F32))
            if h + pair < heads:
                pieces.append(jnp.zeros(((heads - pair - h) * rows, wide), F32))
            placed = jnp.concatenate(pieces, axis=0).astype(BF16)
            keys = k_ref[:, :, cols].reshape(tokens, wide)
            scores = scores + dot(keys, placed, ((1,), (1,)))
            step_scores = step_scores + dot(step_keys[:, cols], placed, ((1,), (1,)))
        halves = split(jnp.where(live, scores.T, 0.0))
        step_halves = split(jnp.where(near, step_scores.T, 0.0))
        for h in range(0, heads, pair):
            cols = slice((top + h) * HEAD_DIM, (top + h) * HEAD_DIM + wide)
            own = slice(h * rows, (h + pair) * rows)
            values = v_ref[:, :, cols].reshape(tokens, wide)
            both = dot(jnp.concatenate([x[own] for x in halves], axis=0), values) + dot(
                jnp.concatenate([x[own] for x in step_halves], axis=0), step_values[:, cols]
            )
            for p in range(pair):
                high = slice(p * rows, (p + 1) * rows)
                low = slice((pair + p) * rows, (pair + p + 1) * rows)
                out_ref[:, head_cols(top + h + p)] = both[high, head_cols(p)] + both[low, head_cols(p)]


def suffix_part(lengths, step_queries, suffix_keys, suffix_values, step_keys, step_values, after):
    samples, suffix, width = suffix_keys.shape
    steps = step_queries.shape[0]
    return pl.pallas_call(
        suffix_kernel,
        in_specs=[SMEM] + [VMEM] * 5 + [ANY] * len(after),
        out_specs=VMEM,
        out_shape=jax.ShapeDtypeStruct((steps * samples, width), F32),
        compiler_params=params(),
        cost_estimate=cost(64 * samples * suffix * width, 4 * samples * suffix * width),
        name="suffix_part",
    )(lengths, step_queries, suffix_keys, suffix_values, step_keys, step_values, *after)


def pick(refs, owner, group, heads):
    wide = heads * HEAD_DIM
    if len(refs) == 1:
        return refs[0][:, pl.ds(pl.multiple_of(owner * wide, wide), wide)]
    each = group // len(refs)
    at = pl.ds(pl.multiple_of(owner % each * wide, wide), wide)
    found = refs[0][:, at]
    for i in range(1, len(refs)):
        found = jnp.where(owner // each == i, refs[i][:, at], found)
    return found


def attended_kernel(group, pieces, top, first, last, q_ref, extra_ref, *refs):
    intra_refs, refs = refs[:pieces], refs[pieces:]
    parts = refs[:group]
    att_ref, raw_ref, sum_ref, acc_ref = refs[-4:]
    rows = q_ref.shape[0]
    heads = parts[0].shape[0]
    dec = extra_ref.shape[0]
    if first:
        acc_ref[...] = jnp.zeros_like(acc_ref)
    else:
        acc_ref[...] = refs[group][...]
    for m in range(group):
        all_cols = owned_cols(group, m, top, heads)
        own_cols = owned_cols(group, m, 0, heads)
        query = q_ref[:, all_cols]
        intra = pick(intra_refs, place(group)[0] ^ m, group, heads)
        extra = extra_ref[:, all_cols]
        squares = acc_ref[:rows, :]
        raw_squares = acc_ref[rows : rows + dec, :]
        atts, raws = [], []
        for h in range(heads):
            cols = head_cols(h)
            att = intra[:, cols] + dot(query[:, cols], parts[m][h, :HEAD_DIM, :].astype(BF16))
            raw = extra[:, cols] + parts[m][h, HEAD_DIM:, :]
            squares = squares + att * att
            raw_squares = raw_squares + raw * raw
            atts.append(att)
            raws.append(raw)
        att_ref[:, own_cols] = jnp.concatenate(atts, axis=1)
        raw_ref[:, own_cols] = jnp.concatenate(raws, axis=1)
        acc_ref[:rows, :] = squares
        acc_ref[rows : rows + dec, :] = raw_squares
    if last:
        sum_ref[...] = jnp.sum(acc_ref[...].T, axis=0, keepdims=True)
    else:
        sum_ref[...] = acc_ref[...]


def attend(chunk, last, queries, intra, extra, parts, before, after):
    group = len(parts)
    heads = parts[0].shape[0]
    wide = group * heads * HEAD_DIM
    rows, dec = queries.shape[0], extra.shape[0]
    pieces = len(intra)
    padded = -(-(rows + dec) // LANES) * LANES
    sums = (1, padded) if last else (padded, LANES)
    return pl.pallas_call(
        functools.partial(attended_kernel, group, pieces, chunk * wide, not before, last),
        in_specs=[VMEM] * (2 + pieces + group + len(before)) + [ANY] * len(after),
        out_specs=[VMEM] * 3,
        out_shape=[
            jax.ShapeDtypeStruct((rows, wide), F32),
            jax.ShapeDtypeStruct((dec, wide), F32),
            jax.ShapeDtypeStruct(sums, F32),
        ],
        scratch_shapes=[pltpu.VMEM((padded, LANES), F32)],
        compiler_params=params(),
        cost_estimate=cost(2 * rows * wide * HEAD_DIM, 10 * rows * wide),
        name="attend",
    )(queries, extra, *intra, *parts, *before, *after)


def norm_kernel(chunks, sums, width, tile, gain_ref, *refs):
    sum_refs = refs[:sums]
    att_refs = refs[sums : sums + chunks]
    raw_refs = refs[sums + chunks : sums + 2 * chunks]
    out_hbm, dec_ref, scale_ref, buf_ref, sems = refs[sums + 2 * chunks :]
    rows, wide = att_refs[0].shape
    dec = raw_refs[0].shape[0]
    samples = dec_ref.shape[1]
    total = sum_refs[0][...]
    for ref in sum_refs[1:]:
        total = total + ref[...]
    scale = lax.rsqrt(total / width + 1e-06)
    scale_ref[...] = jnp.broadcast_to(scale, (LANES, scale.shape[1])).T
    copies = []
    for i in range(rows // tile):
        here = slice(i * tile, (i + 1) * tile)
        row_scale = scale_ref[here, :]
        for c in range(chunks):
            for h in range(wide // HEAD_DIM):
                at = slice(c * wide + h * HEAD_DIM, c * wide + (h + 1) * HEAD_DIM)
                buf_ref[here, at] = (
                    att_refs[c][here, head_cols(h)] * row_scale * gain_ref[:, at]
                ).astype(BF16)
        copies.append(pltpu.make_async_copy(buf_ref.at[here], out_hbm.at[here], sems.at[i]))
        copies[-1].start()
    row_scale = scale_ref[rows : rows + dec, :]
    for c in range(chunks):
        for h in range(wide // HEAD_DIM):
            at = slice(c * wide + h * HEAD_DIM, c * wide + (h + 1) * HEAD_DIM)
            out = raw_refs[c][:, head_cols(h)] * row_scale * gain_ref[:, at]
            for i in range(dec_ref.shape[0]):
                dec_ref[i, :, at] = out[i * samples : (i + 1) * samples].astype(BF16)
    for copy in copies:
        copy.wait()


def normalize(atts, raws, sums, gain, steps, width_all):
    rows, wide = atts[0].shape
    width = wide * len(atts)
    dec = raws[0].shape[0]
    tile = 128 if rows % 128 == 0 else rows
    return pl.pallas_call(
        functools.partial(norm_kernel, len(atts), len(sums), width_all, tile),
        in_specs=[VMEM] * (1 + len(sums) + 2 * len(atts)),
        out_specs=[pl.BlockSpec(memory_space=pltpu.HBM), VMEM],
        out_shape=[
            jax.ShapeDtypeStruct((rows, width), BF16),
            jax.ShapeDtypeStruct((steps, dec // steps, width), BF16),
        ],
        scratch_shapes=[
            pltpu.VMEM((sums[0].shape[1], LANES), F32),
            pltpu.VMEM((rows, width), BF16),
            pltpu.SemaphoreType.DMA((rows // tile,)),
        ],
        compiler_params=params(),
        cost_estimate=cost(0, 6 * rows * width),
        name="normalize",
    )(gain[None, :], *sums, *atts, *raws)


def group_size(devices, heads):
    size = 1
    while (
        devices % (2 * size) == 0
        and size * size < devices
        and heads % (2 * size * CHUNKS) == 0
    ):
        size *= 2
    return size


def on_device(
    queries,
    keys,
    values,
    suffix_keys,
    suffix_values,
    suffix_lengths,
    step_queries,
    step_keys,
    step_values,
    norm_gain,
):
    width = queries.shape[1]
    heads_here = width // HEAD_DIM
    devices = lax.axis_size("seq")
    group = group_size(devices, heads_here)
    blocks = devices // group
    heads = heads_here // (group * CHUNKS)
    def swap(m):
        return [(i, i // group * group + (i % group ^ m)) for i in range(devices)]

    def to_group(messages):
        arrived = list(messages)
        for m in range(group - 1, 0, -1):
            arrived[m] = lax.ppermute(messages[m], "seq", swap(m))
        return arrived

    def across(total):
        return [
            lax.ppermute(total, "seq", [(i, (i + k * group) % devices) for i in range(devices)])
            for k in range(1, blocks)
        ]

    def states(owners, c, after):
        return block_states(owners, c, group, heads, keys, values, step_queries, after)

    def intra(first, wide, after):
        return intra_block(first * HEAD_DIM, wide * HEAD_DIM, queries, keys, values, after)

    half = heads_here // CHUNKS
    first = fetched_states(group - 1, 0, group, heads, keys, values, step_queries)
    rest = states(list(range(group - 1)), 0, [first])
    parts = [to_group([*rest, first])]
    later = states(list(range(group)), 1, [rest[0]])
    parts.append(to_group(later))
    totals = [group_total(parts[0], [later[0]])]
    others = [across(totals[0])]
    intras = [intra(0, half // 2, [totals[0]])]
    totals.append(group_total(parts[1], [intras[0]]))
    others.append(across(totals[1]))
    intras.append(intra(half // 2, half - half // 2, [totals[1]]))
    sent = [priors(parts[0], totals[0], others[0], [intras[1]])]
    entering = [to_group(sent[0])]
    sent.append(priors(parts[1], totals[1], others[1], [sent[0][0]]))
    entering.append(to_group(sent[1]))
    extra = suffix_part(
        suffix_lengths,
        step_queries,
        suffix_keys,
        suffix_values,
        step_keys,
        step_values,
        [sent[1][0]],
    )
    intras = [intras, [intra(half, half, [extra])]]
    atts, raws, sums = [], [], []
    for c in range(CHUNKS):
        att, raw, total = attend(
            c, c == CHUNKS - 1, queries, intras[c], extra, entering[c], sums, []
        )
        sums = [total]
        atts.append(att)
        raws.append(raw)
    sums = sums[0]
    others_of_row = lax.axis_size("head")
    all_sums = [sums] + [
        lax.ppermute(
            sums, "head", [(i, (i + k) % others_of_row) for i in range(others_of_row)]
        )
        for k in range(1, others_of_row)
    ]
    return tuple(
        normalize(
            atts, raws, all_sums, norm_gain, step_queries.shape[0], width * others_of_row
        )
    )


def solution(mesh):
    return jax.shard_map(
        on_device,
        mesh=mesh,
        in_specs=(
            P("seq", "head"),
            P("seq", "head"),
            P("seq", "head"),
            P("seq", None, "head"),
            P("seq", None, "head"),
            P("seq"),
            P(None, "seq", "head"),
            P(None, "seq", "head"),
            P(None, "seq", "head"),
            P("head"),
        ),
        out_specs=(P("seq", "head"), P(None, "seq", "head")),
        check_vma=False,
    )
```

```python
import functools

import jax
import jax.numpy as jnp
from jax import lax
from jax.experimental import pallas as pl
from jax.experimental.pallas import tpu as pltpu
from jax.sharding import PartitionSpec as P

HEAD_DIM = 128
LANES = 128
F32 = jnp.float32
BF16 = jnp.bfloat16
VMEM_LIMIT = 24 * 1024 * 1024
SMEM = pl.BlockSpec(memory_space=pltpu.SMEM)
VMEM = pl.BlockSpec(memory_space=pltpu.VMEM)
ANY = pl.BlockSpec(memory_space=pl.ANY)


def dot(a, b, contract=((1,), (0,))):
    return lax.dot_general(a, b, (contract, ((), ())), preferred_element_type=F32)


def params():
    return pltpu.CompilerParams(vmem_limit_bytes=VMEM_LIMIT)


def cost(flops, moved):
    return pl.CostEstimate(flops=int(flops), bytes_accessed=int(moved), transcendentals=0)


def head_cols(head):
    return slice(head * HEAD_DIM, (head + 1) * HEAD_DIM)


def flat_rows(ref):
    return jnp.concatenate([ref[i].astype(F32) for i in range(ref.shape[0])], axis=0)


def place(group):
    rank = lax.axis_index("seq")
    return lax.rem(rank, group), lax.div(rank, group)


def owned_cols(group, m, each, heads):
    lo, hi = heads
    first = ((place(group)[0] ^ m) * each + lo) * HEAD_DIM
    return pl.ds(pl.multiple_of(first, HEAD_DIM), (hi - lo) * HEAD_DIM)


def split(x):
    high = x.astype(BF16)
    return high, (x - high.astype(F32)).astype(BF16)


def message(out_ref, rows, keys, values):
    for h in range(out_ref.shape[0]):
        cols = head_cols(h)
        out_ref[h, :HEAD_DIM, :] = dot(keys[:, cols], values[:, cols], ((0,), (0,)))
        out_ref[h, HEAD_DIM:, :] = rows[:, cols]


def step_rows(q_ref, cols):
    return jnp.concatenate([q_ref[i, :, cols].astype(F32) for i in range(q_ref.shape[0])], axis=0)


def fetched_state_kernel(group, m, each, heads, q_hbm, k_hbm, v_hbm, out_ref, q_buf, k_buf, v_buf, sems):
    cols = owned_cols(group, m, each, heads)
    copies = [
        pltpu.make_async_copy(k_hbm.at[:, cols], k_buf, sems.at[0]),
        pltpu.make_async_copy(v_hbm.at[:, cols], v_buf, sems.at[1]),
        pltpu.make_async_copy(q_hbm.at[:, :, cols], q_buf, sems.at[2]),
    ]
    for copy in copies:
        copy.start()
    for copy in copies:
        copy.wait()
    message(out_ref, step_rows(q_buf, slice(None)), k_buf[...], v_buf[...])


def fetched_states(m, group, each, heads, keys, values, step_queries):
    rows = keys.shape[0]
    steps, samples, _ = step_queries.shape
    count = heads[1] - heads[0]
    wide = count * HEAD_DIM
    hbm = pl.BlockSpec(memory_space=pltpu.HBM)
    return pl.pallas_call(
        functools.partial(fetched_state_kernel, group, m, each, heads),
        in_specs=[hbm, hbm, hbm],
        out_specs=VMEM,
        out_shape=jax.ShapeDtypeStruct((count, HEAD_DIM + steps * samples, HEAD_DIM), F32),
        scratch_shapes=[
            pltpu.VMEM((steps, samples, wide), step_queries.dtype),
            pltpu.VMEM((rows, wide), keys.dtype),
            pltpu.VMEM((rows, wide), values.dtype),
            pltpu.SemaphoreType.DMA((3,)),
        ],
        compiler_params=params(),
        cost_estimate=cost(2 * rows * wide * HEAD_DIM, 4 * rows * wide),
        name="fetched_states",
    )(
        pltpu.with_memory_space_constraint(step_queries, pltpu.HBM),
        pltpu.with_memory_space_constraint(keys, pltpu.HBM),
        pltpu.with_memory_space_constraint(values, pltpu.HBM),
    )


def state_kernel(group, owners, each, heads, q_ref, k_ref, v_ref, *refs):
    out_refs = refs[-len(owners) :]
    for m, out_ref in zip(owners, out_refs):
        cols = owned_cols(group, m, each, heads)
        message(out_ref, step_rows(q_ref, cols), k_ref[:, cols], v_ref[:, cols])


def block_states(owners, group, each, heads, keys, values, step_queries, after):
    rows = keys.shape[0]
    steps, samples, _ = step_queries.shape
    count = heads[1] - heads[0]
    wide = count * HEAD_DIM
    shape = jax.ShapeDtypeStruct((count, HEAD_DIM + steps * samples, HEAD_DIM), F32)
    return pl.pallas_call(
        functools.partial(state_kernel, group, owners, each, heads),
        in_specs=[VMEM, VMEM, VMEM] + [ANY] * len(after),
        out_specs=[VMEM] * len(owners),
        out_shape=[shape] * len(owners),
        compiler_params=params(),
        cost_estimate=cost(2 * rows * wide * HEAD_DIM * len(owners), 4 * rows * wide * len(owners)),
        name="block_states",
    )(step_queries, keys, values, *after)


def total_kernel(group, heads, *refs):
    here = slice(*heads)
    total = refs[0][here, :HEAD_DIM, :]
    for part in refs[1:group]:
        total = total + part[here, :HEAD_DIM, :]
    refs[-1][...] = total


def group_total(parts, heads, after):
    shape = (heads[1] - heads[0], HEAD_DIM, HEAD_DIM)
    return pl.pallas_call(
        functools.partial(total_kernel, len(parts), heads),
        in_specs=[VMEM] * len(parts) + [ANY] * len(after),
        out_specs=VMEM,
        out_shape=jax.ShapeDtypeStruct(shape, F32),
        compiler_params=params(),
        cost_estimate=cost(0, 4 * shape[0] * HEAD_DIM * HEAD_DIM * (len(parts) + 1)),
        name="group_total",
    )(*parts, *after)


def prior_kernel(owners, group, others, top, *refs):
    parts, total_ref = refs[:group], refs[group]
    other_refs, out_refs = refs[group + 1 : group + 1 + others], refs[-group:]
    here, block = place(group)
    for h in range(total_ref.shape[0]):
        entering = jnp.zeros((HEAD_DIM, HEAD_DIM), F32)
        final = total_ref[h]
        for k in range(others):
            other = other_refs[k][h]
            entering = entering + jnp.where(block > k, other, 0.0)
            final = final + other
        high, low = split(final)
        query = jnp.concatenate([part[top + h, HEAD_DIM:, :] for part in parts], axis=0)
        query = query.astype(BF16)
        raw = dot(query, high) + dot(query, low)
        dec = raw.shape[0] // group
        for m in range(group):
            out_ref = out_refs[owners.index(m)]
            prior = entering
            for k in range(group):
                if k != m:
                    prior = prior + jnp.where(
                        (here ^ k) < (here ^ m), parts[k][top + h, :HEAD_DIM, :], 0.0
                    )
            out_ref[h, :HEAD_DIM, :] = prior
            out_ref[h, HEAD_DIM:, :] = raw[m * dec : (m + 1) * dec]


def priors(owners, parts, top, total, others, after):
    group = len(parts)
    shape = (total.shape[0], *parts[0].shape[1:])
    return pl.pallas_call(
        functools.partial(prior_kernel, owners, group, len(others), top),
        in_specs=[VMEM] * (group + 1 + len(others)) + [ANY] * len(after),
        out_specs=[VMEM] * group,
        out_shape=[jax.ShapeDtypeStruct(shape, F32)] * group,
        compiler_params=params(),
        cost_estimate=cost(0, 4 * total.size * (2 * group + 1 + len(others))),
        name="priors",
    )(*parts, total, *others, *after)


def intra_kernel(tile, heads, q_ref, k_ref, v_ref, *refs):
    out_ref = refs[-1]
    rows, wide = out_ref.shape
    keep = lax.broadcasted_iota(jnp.int32, (tile, tile), 0) >= lax.broadcasted_iota(
        jnp.int32, (tile, tile), 1
    )
    for h, head in enumerate(heads):
        cols = head_cols(head)
        total = None
        for i in range(0, rows, tile):
            scores = dot(q_ref[i:, cols], k_ref[i : i + tile, cols], ((1,), (1,)))
            near = jnp.where(keep, scores[:tile], 0.0).astype(BF16)
            if i + tile < rows:
                near = jnp.concatenate([near, scores[tile:].astype(BF16)], axis=0)
            part = dot(near, v_ref[i : i + tile, cols])
            total = part if total is None else total + part
            out_ref[i : i + tile, head_cols(h)] = total[:tile]
            total = total[tile:]


def intra_block(heads, queries, keys, values, after):
    rows = queries.shape[0]
    wide = len(heads) * HEAD_DIM
    tile = 256 if rows % 256 == 0 else rows
    return pl.pallas_call(
        functools.partial(intra_kernel, tile, heads),
        in_specs=[VMEM] * 3 + [ANY] * len(after),
        out_specs=VMEM,
        out_shape=jax.ShapeDtypeStruct((rows, wide), F32),
        compiler_params=params(),
        cost_estimate=cost(4 * rows * rows * wide, 10 * rows * wide),
        name="intra_block",
    )(queries, keys, values, *after)


def suffix_kernel(lengths_ref, q_ref, k_ref, v_ref, sk_ref, sv_ref, *refs):
    out_ref = refs[-1]
    samples, suffix, width = k_ref.shape
    steps = q_ref.shape[0]
    rows = steps * samples
    tokens = samples * suffix
    heads = max(1, min(LANES // rows, width // HEAD_DIM))
    queries = flat_rows(q_ref)
    step_keys = flat_rows(sk_ref).astype(BF16)
    step_values = flat_rows(sv_ref).astype(BF16)

    at = lax.broadcasted_iota(jnp.int32, (heads * rows, tokens), 0) % samples
    token = lax.broadcasted_iota(jnp.int32, (heads * rows, tokens), 1)
    ends = jnp.zeros((heads * rows, tokens), jnp.int32)
    for n in range(samples):
        ends = jnp.where(at == n, n * suffix + lengths_ref[n], ends)
    live = (token >= at * suffix) & (token < ends)
    row = lax.broadcasted_iota(jnp.int32, (heads * rows, rows), 0) % rows
    col = lax.broadcasted_iota(jnp.int32, (heads * rows, rows), 1)
    near = (row % samples == col % samples) & (row // samples >= col // samples)

    pair = 2 if heads % 2 == 0 else 1
    wide = pair * HEAD_DIM
    for top in range(0, width // HEAD_DIM, heads):
        scores = jnp.zeros((tokens, heads * rows), F32)
        step_scores = jnp.zeros((rows, heads * rows), F32)
        for h in range(0, heads, pair):
            cols = slice((top + h) * HEAD_DIM, (top + h) * HEAD_DIM + wide)
            pieces = []
            for p in range(pair):
                own = [jnp.zeros((rows, HEAD_DIM), F32)] * pair
                own[p] = queries[:, head_cols(top + h + p)]
                pieces.append(jnp.concatenate(own, axis=1))
            if h:
                pieces.insert(0, jnp.zeros((h * rows, wide), F32))
            if h + pair < heads:
                pieces.append(jnp.zeros(((heads - pair - h) * rows, wide), F32))
            placed = jnp.concatenate(pieces, axis=0).astype(BF16)
            keys = k_ref[:, :, cols].reshape(tokens, wide)
            scores = scores + dot(keys, placed, ((1,), (1,)))
            step_scores = step_scores + dot(step_keys[:, cols], placed, ((1,), (1,)))
        halves = split(jnp.where(live, scores.T, 0.0))
        step_halves = split(jnp.where(near, step_scores.T, 0.0))
        for h in range(0, heads, pair):
            cols = slice((top + h) * HEAD_DIM, (top + h) * HEAD_DIM + wide)
            own = slice(h * rows, (h + pair) * rows)
            values = v_ref[:, :, cols].reshape(tokens, wide)
            both = dot(jnp.concatenate([x[own] for x in halves], axis=0), values) + dot(
                jnp.concatenate([x[own] for x in step_halves], axis=0), step_values[:, cols]
            )
            for p in range(pair):
                high = slice(p * rows, (p + 1) * rows)
                low = slice((pair + p) * rows, (pair + p + 1) * rows)
                out_ref[:, head_cols(top + h + p)] = both[high, head_cols(p)] + both[low, head_cols(p)]


def suffix_part(lengths, step_queries, suffix_keys, suffix_values, step_keys, step_values, after):
    samples, suffix, width = suffix_keys.shape
    steps = step_queries.shape[0]
    return pl.pallas_call(
        suffix_kernel,
        in_specs=[SMEM] + [VMEM] * 5 + [ANY] * len(after),
        out_specs=VMEM,
        out_shape=jax.ShapeDtypeStruct((steps * samples, width), F32),
        compiler_params=params(),
        cost_estimate=cost(64 * samples * suffix * width, 4 * samples * suffix * width),
        name="suffix_part",
    )(lengths, step_queries, suffix_keys, suffix_values, step_keys, step_values, *after)


def attended_kernel(group, pieces, each, heads, first, last, q_ref, extra_ref, *refs):
    intra_refs, refs = refs[:pieces], refs[pieces:]
    parts = refs[:group]
    att_ref, raw_ref, sum_ref, acc_ref = refs[-4:]
    rows = q_ref.shape[0]
    dec = extra_ref.shape[0]
    count = heads[1] - heads[0]
    if first:
        acc_ref[...] = jnp.zeros_like(acc_ref)
    else:
        acc_ref[...] = refs[group][...]
    for m in range(group):
        all_cols = owned_cols(group, m, each, heads)
        own_cols = owned_cols(group, m, count, (0, count))
        query = q_ref[:, all_cols]
        extra = extra_ref[:, all_cols]
        if pieces == 1:
            intra = intra_refs[0][:, own_cols]
        else:
            owner = place(group)[0] ^ m
            share = group // pieces
            at = pl.multiple_of(lax.rem(owner, share) * count * HEAD_DIM, HEAD_DIM)
            intra = intra_refs[0][:, pl.ds(at, count * HEAD_DIM)]
            for i in range(1, pieces):
                intra = jnp.where(
                    lax.div(owner, share) == i, intra_refs[i][:, pl.ds(at, count * HEAD_DIM)], intra
                )
        squares = acc_ref[:rows, :]
        raw_squares = acc_ref[rows : rows + dec, :]
        atts, raws = [], []
        for h in range(count):
            cols = head_cols(h)
            att = intra[:, cols] + dot(query[:, cols], parts[m][h, :HEAD_DIM, :].astype(BF16))
            raw = extra[:, cols] + parts[m][h, HEAD_DIM:, :]
            squares = squares + att * att
            raw_squares = raw_squares + raw * raw
            atts.append(att)
            raws.append(raw)
        att_ref[:, own_cols] = jnp.concatenate(atts, axis=1)
        raw_ref[:, own_cols] = jnp.concatenate(raws, axis=1)
        acc_ref[:rows, :] = squares
        acc_ref[rows : rows + dec, :] = raw_squares
    if last:
        sum_ref[...] = jnp.sum(acc_ref[...].T, axis=0, keepdims=True)
    else:
        sum_ref[...] = acc_ref[...]


def attend(each, heads, last, queries, intra, extra, parts, before, after):
    group = len(parts)
    wide = group * (heads[1] - heads[0]) * HEAD_DIM
    rows, dec = queries.shape[0], extra.shape[0]
    pieces = len(intra)
    padded = -(-(rows + dec) // LANES) * LANES
    sums = (1, padded) if last else (padded, LANES)
    return pl.pallas_call(
        functools.partial(attended_kernel, group, pieces, each, heads, not before, last),
        in_specs=[VMEM] * (2 + pieces + group + len(before)) + [ANY] * len(after),
        out_specs=[VMEM] * 3,
        out_shape=[
            jax.ShapeDtypeStruct((rows, wide), F32),
            jax.ShapeDtypeStruct((dec, wide), F32),
            jax.ShapeDtypeStruct(sums, F32),
        ],
        scratch_shapes=[pltpu.VMEM((padded, LANES), F32)],
        compiler_params=params(),
        cost_estimate=cost(2 * rows * wide * HEAD_DIM, 10 * rows * wide),
        name="attend",
    )(queries, extra, *intra, *parts, *before, *after)


def norm_kernel(heads, sums, width, tile, gain_ref, *refs):
    chunks = len(heads)
    sum_refs = refs[:sums]
    att_refs = refs[sums : sums + chunks]
    raw_refs = refs[sums + chunks : sums + 2 * chunks]
    out_hbm, dec_hbm, scale_ref, buf_ref, dec_ref, sems = refs[sums + 2 * chunks :]
    rows = att_refs[0].shape[0]
    dec = raw_refs[0].shape[0]
    samples = dec_ref.shape[1]
    total = sum_refs[0][...]
    for ref in sum_refs[1:]:
        total = total + ref[...]
    scale = lax.rsqrt(total / width + 1e-06)
    scale_ref[...] = jnp.broadcast_to(scale, (LANES, scale.shape[1])).T
    copies = []
    for i in range(rows // tile):
        here = slice(i * tile, (i + 1) * tile)
        row_scale = scale_ref[here, :]
        for c in range(chunks):
            for h, head in enumerate(heads[c]):
                at = head_cols(head)
                buf_ref[here, at] = (
                    att_refs[c][here, head_cols(h)] * row_scale * gain_ref[:, at]
                ).astype(BF16)
        copies.append(pltpu.make_async_copy(buf_ref.at[here], out_hbm.at[here], sems.at[i]))
        copies[-1].start()
        if i == 0:
            row_scale = scale_ref[rows : rows + dec, :]
            for c in range(chunks):
                for h, head in enumerate(heads[c]):
                    at = head_cols(head)
                    out = raw_refs[c][:, head_cols(h)] * row_scale * gain_ref[:, at]
                    for j in range(dec_ref.shape[0]):
                        dec_ref[j, :, at] = out[j * samples : (j + 1) * samples].astype(BF16)
            copies.append(pltpu.make_async_copy(dec_ref, dec_hbm, sems.at[rows // tile]))
            copies[-1].start()
    for copy in copies:
        copy.wait()


def normalize(heads, atts, raws, sums, gain, steps, width_all):
    rows, width = atts[0].shape[0], gain.shape[0]
    dec = raws[0].shape[0]
    tile = 128 if rows % 128 == 0 else rows
    return pl.pallas_call(
        functools.partial(norm_kernel, heads, len(sums), width_all, tile),
        in_specs=[VMEM] * (1 + len(sums) + 2 * len(atts)),
        out_specs=[pl.BlockSpec(memory_space=pltpu.HBM)] * 2,
        out_shape=[
            jax.ShapeDtypeStruct((rows, width), BF16),
            jax.ShapeDtypeStruct((steps, dec // steps, width), BF16),
        ],
        scratch_shapes=[
            pltpu.VMEM((sums[0].shape[1], LANES), F32),
            pltpu.VMEM((rows, width), BF16),
            pltpu.VMEM((steps, dec // steps, width), BF16),
            pltpu.SemaphoreType.DMA((rows // tile + 1,)),
        ],
        compiler_params=params(),
        cost_estimate=cost(0, 6 * rows * width),
        name="normalize",
    )(gain[None, :], *sums, *atts, *raws)


SENT = (1, 1)
DONE = (1, 1)
ORDER = "s0 s1 t0 i0.0 i0.1 p0 t1 x p1 i1 a0 a1"
PIECES = (2, 1)
FIRST = 1
RANKING = lambda m: m


def group_size(devices, heads):
    size = 1
    while devices % (2 * size) == 0 and size * size < devices and heads % (4 * size) == 0:
        size *= 2
    return size


def bounds(shares, heads):
    marks = [0]
    for i in range(len(shares)):
        marks.append(heads * sum(shares[: i + 1]) // sum(shares))
    return list(zip(marks[:-1], marks[1:]))


def on_device(
    queries,
    keys,
    values,
    suffix_keys,
    suffix_values,
    suffix_lengths,
    step_queries,
    step_keys,
    step_values,
    norm_gain,
):
    width = queries.shape[1]
    heads_here = width // HEAD_DIM
    devices = lax.axis_size("seq")
    group = group_size(devices, heads_here)
    blocks = devices // group
    each = heads_here // group
    fine = each % sum(DONE) == 0 and each % sum(SENT) == 0
    sent_heads, done_heads = (bounds(SENT, each), bounds(DONE, each)) if fine else (
        bounds((1, 1), each),
        bounds((1, 1), each),
    )
    chunk_heads = [
        [owner * each + h for owner in range(group) for h in range(lo, hi)] for lo, hi in done_heads
    ]

    def swap(messages):
        return [messages[0]] + [
            lax.ppermute(
                messages[m],
                "seq",
                [(i, i // group * group + (i % group ^ m)) for i in range(devices)],
            )
            for m in range(1, group)
        ]

    owners = sorted(range(group), key=RANKING)

    def ordered(owners, messages):
        made = dict(zip(owners, messages))
        return [made[m] for m in range(group)]

    def across(total):
        return [
            lax.ppermute(total, "seq", [(i, (i + k * group) % devices) for i in range(devices)])
            for k in range(1, blocks)
        ]

    def holder(c):
        lo, hi = done_heads[c]
        for i, (start, end) in enumerate(sent_heads):
            if start <= lo and hi <= end:
                return i, lo - start

    parts, totals, others, entering, intras, atts, raws = {}, {}, {}, {}, {}, {}, {}
    extra, sums, last = None, [], []
    for step in ORDER.split():
        kind, c = step[0], int(step[1:].split(".")[0] or 0) if len(step) > 1 else 0
        if kind == "s" and c < len(sent_heads):
            if c == 0:
                m = FIRST % group
                given = (group, each, sent_heads[0], keys, values, step_queries)
                first = fetched_states(m, *given)
                rest = block_states([i for i in owners if i != m], *given, [first])
                messages = ordered([m] + [i for i in owners if i != m], [first, *rest])
                last = [rest[0]]
            else:
                messages = block_states(
                    owners,
                    group,
                    each,
                    sent_heads[c],
                    keys,
                    values,
                    step_queries,
                    last,
                )
                last = [messages[0]]
                messages = ordered(owners, messages)
            parts[c] = swap(messages)
        elif kind == "t" and c < len(done_heads):
            i, top = holder(c)
            count = done_heads[c][1] - done_heads[c][0]
            totals[c] = group_total(parts[i], (top, top + count), last)
            others[c] = across(totals[c])
            last = [totals[c]]
        elif kind == "p" and c < len(done_heads):
            i, top = holder(c)
            messages = priors(owners, parts[i], top, totals[c], others[c], last)
            entering[c] = swap(ordered(owners, messages))
            last = [messages[0]]
        elif kind == "i" and c < len(done_heads):
            heads = chunk_heads[c]
            if "." in step:
                share = len(heads) // PIECES[c]
                piece = int(step.split(".")[1])
                heads = heads[piece * share : (piece + 1) * share]
            intras.setdefault(c, []).append(intra_block(heads, queries, keys, values, last))
            last = [intras[c][-1]]
        elif kind == "x":
            extra = suffix_part(
                suffix_lengths,
                step_queries,
                suffix_keys,
                suffix_values,
                step_keys,
                step_values,
                last,
            )
            last = [extra]
        elif kind == "a" and c < len(done_heads):
            atts[c], raws[c], total = attend(
                each,
                done_heads[c],
                c == len(done_heads) - 1,
                queries,
                intras[c],
                extra,
                entering[c],
                sums,
                [],
            )
            sums = [total]
    row = lax.axis_size("head")
    step = (lambda i, k: i ^ k) if row & (row - 1) == 0 else (lambda i, k: (i + k) % row)
    all_sums = sums + [
        lax.ppermute(sums[0], "head", [(i, step(i, k)) for i in range(row)]) for k in range(1, row)
    ]
    return tuple(
        normalize(
            chunk_heads,
            [atts[c] for c in range(len(done_heads))],
            [raws[c] for c in range(len(done_heads))],
            all_sums,
            norm_gain,
            step_queries.shape[0],
            width * row,
        )
    )


def solution(mesh):
    return jax.shard_map(
        on_device,
        mesh=mesh,
        in_specs=(
            P("seq", "head"),
            P("seq", "head"),
            P("seq", "head"),
            P("seq", None, "head"),
            P("seq", None, "head"),
            P("seq"),
            P(None, "seq", "head"),
            P(None, "seq", "head"),
            P(None, "seq", "head"),
            P("head"),
        ),
        out_specs=(P("seq", "head"), P(None, "seq", "head")),
        check_vma=False,
    )
```

```python
import functools

import jax
import jax.numpy as jnp
from jax import lax
from jax.experimental import pallas as pl
from jax.experimental.pallas import tpu as pltpu
from jax.sharding import PartitionSpec as P

HEAD_DIM = 128
LANES = 128
F32 = jnp.float32
BF16 = jnp.bfloat16
VMEM_LIMIT = 24 * 1024 * 1024
SMEM = pl.BlockSpec(memory_space=pltpu.SMEM)
VMEM = pl.BlockSpec(memory_space=pltpu.VMEM)
ANY = pl.BlockSpec(memory_space=pl.ANY)


def dot(a, b, contract=((1,), (0,))):
    return lax.dot_general(a, b, (contract, ((), ())), preferred_element_type=F32)


def params():
    return pltpu.CompilerParams(vmem_limit_bytes=VMEM_LIMIT)


def cost(flops, moved):
    return pl.CostEstimate(flops=int(flops), bytes_accessed=int(moved), transcendentals=0)


def head_cols(head):
    return slice(head * HEAD_DIM, (head + 1) * HEAD_DIM)


def flat_rows(ref):
    return jnp.concatenate([ref[i].astype(F32) for i in range(ref.shape[0])], axis=0)


def place(group):
    rank = lax.axis_index("seq")
    return lax.rem(rank, group), lax.div(rank, group)


def owned_cols(group, m, each, heads):
    lo, hi = heads
    first = ((place(group)[0] ^ m) * each + lo) * HEAD_DIM
    return pl.ds(pl.multiple_of(first, HEAD_DIM), (hi - lo) * HEAD_DIM)


def split(x):
    high = x.astype(BF16)
    return high, (x - high.astype(F32)).astype(BF16)


def message(out_ref, rows, keys, values):
    for h in range(out_ref.shape[0]):
        cols = head_cols(h)
        out_ref[h, :HEAD_DIM, :] = dot(keys[:, cols], values[:, cols], ((0,), (0,)))
        out_ref[h, HEAD_DIM:, :] = rows[:, cols]


def step_rows(q_ref, cols):
    return jnp.concatenate([q_ref[i, :, cols].astype(F32) for i in range(q_ref.shape[0])], axis=0)


def fetched_state_kernel(group, m, each, heads, q_hbm, k_hbm, v_hbm, out_ref, q_buf, k_buf, v_buf, sems):
    cols = owned_cols(group, m, each, heads)
    copies = [
        pltpu.make_async_copy(k_hbm.at[:, cols], k_buf, sems.at[0]),
        pltpu.make_async_copy(v_hbm.at[:, cols], v_buf, sems.at[1]),
        pltpu.make_async_copy(q_hbm.at[:, :, cols], q_buf, sems.at[2]),
    ]
    for copy in copies:
        copy.start()
    for copy in copies:
        copy.wait()
    message(out_ref, step_rows(q_buf, slice(None)), k_buf[...], v_buf[...])


def fetched_states(m, group, each, heads, keys, values, step_queries):
    rows = keys.shape[0]
    steps, samples, _ = step_queries.shape
    count = heads[1] - heads[0]
    wide = count * HEAD_DIM
    hbm = pl.BlockSpec(memory_space=pltpu.HBM)
    return pl.pallas_call(
        functools.partial(fetched_state_kernel, group, m, each, heads),
        in_specs=[hbm, hbm, hbm],
        out_specs=VMEM,
        out_shape=jax.ShapeDtypeStruct((count, HEAD_DIM + steps * samples, HEAD_DIM), F32),
        scratch_shapes=[
            pltpu.VMEM((steps, samples, wide), step_queries.dtype),
            pltpu.VMEM((rows, wide), keys.dtype),
            pltpu.VMEM((rows, wide), values.dtype),
            pltpu.SemaphoreType.DMA((3,)),
        ],
        compiler_params=params(),
        cost_estimate=cost(2 * rows * wide * HEAD_DIM, 4 * rows * wide),
        name="fetched_states",
    )(
        pltpu.with_memory_space_constraint(step_queries, pltpu.HBM),
        pltpu.with_memory_space_constraint(keys, pltpu.HBM),
        pltpu.with_memory_space_constraint(values, pltpu.HBM),
    )


def state_kernel(group, owners, each, heads, q_ref, k_ref, v_ref, *refs):
    out_refs = refs[-len(owners) :]
    for m, out_ref in zip(owners, out_refs):
        cols = owned_cols(group, m, each, heads)
        message(out_ref, step_rows(q_ref, cols), k_ref[:, cols], v_ref[:, cols])


def block_states(owners, group, each, heads, keys, values, step_queries, after):
    rows = keys.shape[0]
    steps, samples, _ = step_queries.shape
    count = heads[1] - heads[0]
    wide = count * HEAD_DIM
    shape = jax.ShapeDtypeStruct((count, HEAD_DIM + steps * samples, HEAD_DIM), F32)
    return pl.pallas_call(
        functools.partial(state_kernel, group, owners, each, heads),
        in_specs=[VMEM, VMEM, VMEM] + [ANY] * len(after),
        out_specs=[VMEM] * len(owners),
        out_shape=[shape] * len(owners),
        compiler_params=params(),
        cost_estimate=cost(2 * rows * wide * HEAD_DIM * len(owners), 4 * rows * wide * len(owners)),
        name="block_states",
    )(step_queries, keys, values, *after)


def total_kernel(group, heads, *refs):
    here = slice(*heads)
    total = refs[0][here, :HEAD_DIM, :]
    for part in refs[1:group]:
        total = total + part[here, :HEAD_DIM, :]
    refs[-1][...] = total


def group_total(parts, heads, after):
    shape = (heads[1] - heads[0], HEAD_DIM, HEAD_DIM)
    return pl.pallas_call(
        functools.partial(total_kernel, len(parts), heads),
        in_specs=[VMEM] * len(parts) + [ANY] * len(after),
        out_specs=VMEM,
        out_shape=jax.ShapeDtypeStruct(shape, F32),
        compiler_params=params(),
        cost_estimate=cost(0, 4 * shape[0] * HEAD_DIM * HEAD_DIM * (len(parts) + 1)),
        name="group_total",
    )(*parts, *after)


def prior_kernel(owners, group, others, top, *refs):
    parts, total_ref = refs[:group], refs[group]
    other_refs, out_refs = refs[group + 1 : group + 1 + others], refs[-group:]
    here, block = place(group)
    for h in range(total_ref.shape[0]):
        entering = jnp.zeros((HEAD_DIM, HEAD_DIM), F32)
        final = total_ref[h]
        for k in range(others):
            other = other_refs[k][h]
            entering = entering + jnp.where(block > k, other, 0.0)
            final = final + other
        high, low = split(final)
        query = jnp.concatenate([part[top + h, HEAD_DIM:, :] for part in parts], axis=0)
        query = query.astype(BF16)
        raw = dot(query, high) + dot(query, low)
        dec = raw.shape[0] // group
        for m in range(group):
            out_ref = out_refs[owners.index(m)]
            prior = entering
            for k in range(group):
                if k != m:
                    prior = prior + jnp.where(
                        (here ^ k) < (here ^ m), parts[k][top + h, :HEAD_DIM, :], 0.0
                    )
            out_ref[h, :HEAD_DIM, :] = prior
            out_ref[h, HEAD_DIM:, :] = raw[m * dec : (m + 1) * dec]


def priors(owners, parts, top, total, others, after):
    group = len(parts)
    shape = (total.shape[0], *parts[0].shape[1:])
    return pl.pallas_call(
        functools.partial(prior_kernel, owners, group, len(others), top),
        in_specs=[VMEM] * (group + 1 + len(others)) + [ANY] * len(after),
        out_specs=[VMEM] * group,
        out_shape=[jax.ShapeDtypeStruct(shape, F32)] * group,
        compiler_params=params(),
        cost_estimate=cost(0, 4 * total.size * (2 * group + 1 + len(others))),
        name="priors",
    )(*parts, total, *others, *after)


def intra_kernel(tile, heads, q_ref, k_ref, v_ref, *refs):
    out_ref = refs[-1]
    rows, wide = out_ref.shape
    keep = lax.broadcasted_iota(jnp.int32, (tile, tile), 0) >= lax.broadcasted_iota(
        jnp.int32, (tile, tile), 1
    )
    for h, head in enumerate(heads):
        cols = head_cols(head)
        total = None
        for i in range(0, rows, tile):
            scores = dot(q_ref[i:, cols], k_ref[i : i + tile, cols], ((1,), (1,)))
            near = jnp.where(keep, scores[:tile], 0.0).astype(BF16)
            if i + tile < rows:
                near = jnp.concatenate([near, scores[tile:].astype(BF16)], axis=0)
            part = dot(near, v_ref[i : i + tile, cols])
            total = part if total is None else total + part
            out_ref[i : i + tile, head_cols(h)] = total[:tile]
            total = total[tile:]


def intra_block(heads, queries, keys, values, after):
    rows = queries.shape[0]
    wide = len(heads) * HEAD_DIM
    tile = 256 if rows % 256 == 0 else rows
    return pl.pallas_call(
        functools.partial(intra_kernel, tile, heads),
        in_specs=[VMEM] * 3 + [ANY] * len(after),
        out_specs=VMEM,
        out_shape=jax.ShapeDtypeStruct((rows, wide), F32),
        compiler_params=params(),
        cost_estimate=cost(4 * rows * rows * wide, 10 * rows * wide),
        name="intra_block",
    )(queries, keys, values, *after)


def suffix_kernel(lengths_ref, q_ref, k_ref, v_ref, sk_ref, sv_ref, *refs):
    out_ref = refs[-1]
    samples, suffix, width = k_ref.shape
    steps = q_ref.shape[0]
    rows = steps * samples
    tokens = samples * suffix
    heads = max(1, min(LANES // rows, width // HEAD_DIM))
    queries = flat_rows(q_ref)
    step_keys = flat_rows(sk_ref).astype(BF16)
    step_values = flat_rows(sv_ref).astype(BF16)

    at = lax.broadcasted_iota(jnp.int32, (heads * rows, tokens), 0) % samples
    token = lax.broadcasted_iota(jnp.int32, (heads * rows, tokens), 1)
    ends = jnp.zeros((heads * rows, tokens), jnp.int32)
    for n in range(samples):
        ends = jnp.where(at == n, n * suffix + lengths_ref[n], ends)
    live = (token >= at * suffix) & (token < ends)
    row = lax.broadcasted_iota(jnp.int32, (heads * rows, rows), 0) % rows
    col = lax.broadcasted_iota(jnp.int32, (heads * rows, rows), 1)
    near = (row % samples == col % samples) & (row // samples >= col // samples)

    pair = 2 if heads % 2 == 0 else 1
    wide = pair * HEAD_DIM
    for top in range(0, width // HEAD_DIM, heads):
        scores = jnp.zeros((tokens, heads * rows), F32)
        step_scores = jnp.zeros((rows, heads * rows), F32)
        for h in range(0, heads, pair):
            cols = slice((top + h) * HEAD_DIM, (top + h) * HEAD_DIM + wide)
            pieces = []
            for p in range(pair):
                own = [jnp.zeros((rows, HEAD_DIM), F32)] * pair
                own[p] = queries[:, head_cols(top + h + p)]
                pieces.append(jnp.concatenate(own, axis=1))
            if h:
                pieces.insert(0, jnp.zeros((h * rows, wide), F32))
            if h + pair < heads:
                pieces.append(jnp.zeros(((heads - pair - h) * rows, wide), F32))
            placed = jnp.concatenate(pieces, axis=0).astype(BF16)
            keys = k_ref[:, :, cols].reshape(tokens, wide)
            scores = scores + dot(keys, placed, ((1,), (1,)))
            step_scores = step_scores + dot(step_keys[:, cols], placed, ((1,), (1,)))
        halves = split(jnp.where(live, scores.T, 0.0))
        step_halves = split(jnp.where(near, step_scores.T, 0.0))
        for h in range(0, heads, pair):
            cols = slice((top + h) * HEAD_DIM, (top + h) * HEAD_DIM + wide)
            own = slice(h * rows, (h + pair) * rows)
            values = v_ref[:, :, cols].reshape(tokens, wide)
            both = dot(jnp.concatenate([x[own] for x in halves], axis=0), values) + dot(
                jnp.concatenate([x[own] for x in step_halves], axis=0), step_values[:, cols]
            )
            for p in range(pair):
                high = slice(p * rows, (p + 1) * rows)
                low = slice((pair + p) * rows, (pair + p + 1) * rows)
                out_ref[:, head_cols(top + h + p)] = both[high, head_cols(p)] + both[low, head_cols(p)]


def suffix_part(lengths, step_queries, suffix_keys, suffix_values, step_keys, step_values, after):
    samples, suffix, width = suffix_keys.shape
    steps = step_queries.shape[0]
    return pl.pallas_call(
        suffix_kernel,
        in_specs=[SMEM] + [VMEM] * 5 + [ANY] * len(after),
        out_specs=VMEM,
        out_shape=jax.ShapeDtypeStruct((steps * samples, width), F32),
        compiler_params=params(),
        cost_estimate=cost(64 * samples * suffix * width, 4 * samples * suffix * width),
        name="suffix_part",
    )(lengths, step_queries, suffix_keys, suffix_values, step_keys, step_values, *after)


def attended_kernel(group, pieces, each, heads, first, last, q_ref, extra_ref, *refs):
    intra_refs, refs = refs[:pieces], refs[pieces:]
    parts = refs[:group]
    att_ref, raw_ref, sum_ref, acc_ref = refs[-4:]
    rows = q_ref.shape[0]
    dec = extra_ref.shape[0]
    count = heads[1] - heads[0]
    if first:
        acc_ref[...] = jnp.zeros_like(acc_ref)
    else:
        acc_ref[...] = refs[group][...]
    for m in range(group):
        all_cols = owned_cols(group, m, each, heads)
        own_cols = owned_cols(group, m, count, (0, count))
        query = q_ref[:, all_cols]
        extra = extra_ref[:, all_cols]
        if pieces == 1:
            intra = intra_refs[0][:, own_cols]
        else:
            owner = place(group)[0] ^ m
            share = group // pieces
            at = pl.multiple_of(lax.rem(owner, share) * count * HEAD_DIM, HEAD_DIM)
            intra = intra_refs[0][:, pl.ds(at, count * HEAD_DIM)]
            for i in range(1, pieces):
                intra = jnp.where(
                    lax.div(owner, share) == i, intra_refs[i][:, pl.ds(at, count * HEAD_DIM)], intra
                )
        squares = acc_ref[:rows, :]
        raw_squares = acc_ref[rows : rows + dec, :]
        atts, raws = [], []
        for h in range(count):
            cols = head_cols(h)
            att = intra[:, cols] + dot(query[:, cols], parts[m][h, :HEAD_DIM, :].astype(BF16))
            raw = extra[:, cols] + parts[m][h, HEAD_DIM:, :]
            squares = squares + att * att
            raw_squares = raw_squares + raw * raw
            atts.append(att)
            raws.append(raw)
        att_ref[:, own_cols] = jnp.concatenate(atts, axis=1)
        raw_ref[:, own_cols] = jnp.concatenate(raws, axis=1)
        acc_ref[:rows, :] = squares
        acc_ref[rows : rows + dec, :] = raw_squares
    if last:
        sum_ref[...] = jnp.sum(acc_ref[...].T, axis=0, keepdims=True)
    else:
        sum_ref[...] = acc_ref[...]


def attend(each, heads, last, queries, intra, extra, parts, before, after):
    group = len(parts)
    wide = group * (heads[1] - heads[0]) * HEAD_DIM
    rows, dec = queries.shape[0], extra.shape[0]
    pieces = len(intra)
    padded = -(-(rows + dec) // LANES) * LANES
    sums = (1, padded) if last else (padded, LANES)
    return pl.pallas_call(
        functools.partial(attended_kernel, group, pieces, each, heads, not before, last),
        in_specs=[VMEM] * (2 + pieces + group + len(before)) + [ANY] * len(after),
        out_specs=[VMEM] * 3,
        out_shape=[
            jax.ShapeDtypeStruct((rows, wide), F32),
            jax.ShapeDtypeStruct((dec, wide), F32),
            jax.ShapeDtypeStruct(sums, F32),
        ],
        scratch_shapes=[pltpu.VMEM((padded, LANES), F32)],
        compiler_params=params(),
        cost_estimate=cost(2 * rows * wide * HEAD_DIM, 10 * rows * wide),
        name="attend",
    )(queries, extra, *intra, *parts, *before, *after)


def norm_kernel(heads, sums, width, tile, gain_ref, *refs):
    chunks = len(heads)
    sum_refs = refs[:sums]
    att_refs = refs[sums : sums + chunks]
    raw_refs = refs[sums + chunks : sums + 2 * chunks]
    out_hbm, dec_hbm, scale_ref, buf_ref, dec_ref, sems = refs[sums + 2 * chunks :]
    rows = att_refs[0].shape[0]
    dec = raw_refs[0].shape[0]
    samples = dec_ref.shape[1]
    total = sum_refs[0][...]
    for ref in sum_refs[1:]:
        total = total + ref[...]
    scale = lax.rsqrt(total / width + 1e-06)
    scale_ref[...] = jnp.broadcast_to(scale, (LANES, scale.shape[1])).T
    copies = []
    for i in range(rows // tile):
        here = slice(i * tile, (i + 1) * tile)
        row_scale = scale_ref[here, :]
        for c in range(chunks):
            for h, head in enumerate(heads[c]):
                at = head_cols(head)
                buf_ref[here, at] = (
                    att_refs[c][here, head_cols(h)] * row_scale * gain_ref[:, at]
                ).astype(BF16)
        copies.append(pltpu.make_async_copy(buf_ref.at[here], out_hbm.at[here], sems.at[i]))
        copies[-1].start()
        if i == 0:
            row_scale = scale_ref[rows : rows + dec, :]
            for c in range(chunks):
                for h, head in enumerate(heads[c]):
                    at = head_cols(head)
                    out = raw_refs[c][:, head_cols(h)] * row_scale * gain_ref[:, at]
                    for j in range(dec_ref.shape[0]):
                        dec_ref[j, :, at] = out[j * samples : (j + 1) * samples].astype(BF16)
            copies.append(pltpu.make_async_copy(dec_ref, dec_hbm, sems.at[rows // tile]))
            copies[-1].start()
    for copy in copies:
        copy.wait()


def normalize(heads, atts, raws, sums, gain, steps, width_all):
    rows, width = atts[0].shape[0], gain.shape[0]
    dec = raws[0].shape[0]
    tile = 128 if rows % 128 == 0 else rows
    return pl.pallas_call(
        functools.partial(norm_kernel, heads, len(sums), width_all, tile),
        in_specs=[VMEM] * (1 + len(sums) + 2 * len(atts)),
        out_specs=[pl.BlockSpec(memory_space=pltpu.HBM)] * 2,
        out_shape=[
            jax.ShapeDtypeStruct((rows, width), BF16),
            jax.ShapeDtypeStruct((steps, dec // steps, width), BF16),
        ],
        scratch_shapes=[
            pltpu.VMEM((sums[0].shape[1], LANES), F32),
            pltpu.VMEM((rows, width), BF16),
            pltpu.VMEM((steps, dec // steps, width), BF16),
            pltpu.SemaphoreType.DMA((rows // tile + 1,)),
        ],
        compiler_params=params(),
        cost_estimate=cost(0, 6 * rows * width),
        name="normalize",
    )(gain[None, :], *sums, *atts, *raws)


SENT = (1, 1)
DONE = (1, 1)
ORDER = ("s0", "s1", "t0", "i0.0", "i0.1", "p0", "t1", "x", "p1", "i1", "a0", "a1")
PIECES = (2, 1)


def group_size(devices, heads):
    size = 1
    while devices % (2 * size) == 0 and size * size < devices and heads % (4 * size) == 0:
        size *= 2
    return size


def bounds(shares, heads):
    marks = [0]
    for i in range(len(shares)):
        marks.append(heads * sum(shares[: i + 1]) // sum(shares))
    return list(zip(marks[:-1], marks[1:]))


def on_device(
    queries,
    keys,
    values,
    suffix_keys,
    suffix_values,
    suffix_lengths,
    step_queries,
    step_keys,
    step_values,
    norm_gain,
):
    width = queries.shape[1]
    heads_here = width // HEAD_DIM
    devices = lax.axis_size("seq")
    group = group_size(devices, heads_here)
    blocks = devices // group
    each = heads_here // group
    fine = each % sum(DONE) == 0 and each % sum(SENT) == 0
    sent_heads, done_heads = (bounds(SENT, each), bounds(DONE, each)) if fine else (
        bounds((1, 1), each),
        bounds((1, 1), each),
    )
    chunk_heads = [
        [owner * each + h for owner in range(group) for h in range(lo, hi)] for lo, hi in done_heads
    ]

    def swap(messages):
        return [messages[0]] + [
            lax.ppermute(
                messages[m],
                "seq",
                [(i, i // group * group + (i % group ^ m)) for i in range(devices)],
            )
            for m in range(1, group)
        ]

    owners = list(range(group))[::-1]

    def ordered(owners, messages):
        made = dict(zip(owners, messages))
        return [made[m] for m in range(group)]

    def across(total):
        return [
            lax.ppermute(total, "seq", [(i, (i + k * group) % devices) for i in range(devices)])
            for k in range(1, blocks)
        ]

    def holder(c):
        lo, hi = done_heads[c]
        for i, (start, end) in enumerate(sent_heads):
            if start <= lo and hi <= end:
                return i, lo - start

    parts, totals, others, entering, intras, atts, raws = {}, {}, {}, {}, {}, {}, {}
    extra, sums, last = None, [], []
    for step in ORDER:
        kind, c = step[0], int(step[1:].split(".")[0] or 0) if len(step) > 1 else 0
        if kind == "s" and c < len(sent_heads):
            if c == 0:
                m = owners[0]
                given = (group, each, sent_heads[0], keys, values, step_queries)
                first = fetched_states(m, *given)
                rest = block_states([i for i in owners if i != m], *given, [first])
                messages = ordered([m] + [i for i in owners if i != m], [first, *rest])
                last = [rest[0]]
            else:
                messages = block_states(
                    owners,
                    group,
                    each,
                    sent_heads[c],
                    keys,
                    values,
                    step_queries,
                    last,
                )
                last = [messages[0]]
                messages = ordered(owners, messages)
            parts[c] = swap(messages)
        elif kind == "t" and c < len(done_heads):
            i, top = holder(c)
            count = done_heads[c][1] - done_heads[c][0]
            totals[c] = group_total(parts[i], (top, top + count), last)
            others[c] = across(totals[c])
            last = [totals[c]]
        elif kind == "p" and c < len(done_heads):
            i, top = holder(c)
            messages = priors(owners, parts[i], top, totals[c], others[c], last)
            entering[c] = swap(ordered(owners, messages))
            last = [messages[0]]
        elif kind == "i" and c < len(done_heads):
            heads = chunk_heads[c]
            if "." in step:
                share = len(heads) // PIECES[c]
                piece = int(step.split(".")[1])
                heads = heads[piece * share : (piece + 1) * share]
            intras.setdefault(c, []).append(intra_block(heads, queries, keys, values, last))
            last = [intras[c][-1]]
        elif kind == "x":
            extra = suffix_part(
                suffix_lengths,
                step_queries,
                suffix_keys,
                suffix_values,
                step_keys,
                step_values,
                last,
            )
            last = [extra]
        elif kind == "a" and c < len(done_heads):
            atts[c], raws[c], total = attend(
                each,
                done_heads[c],
                c == len(done_heads) - 1,
                queries,
                intras[c],
                extra,
                entering[c],
                sums,
                [],
            )
            sums = [total]
    row = lax.axis_size("head")
    step = (lambda i, k: i ^ k) if row & (row - 1) == 0 else (lambda i, k: (i + k) % row)
    all_sums = sums + [
        lax.ppermute(sums[0], "head", [(i, step(i, k)) for i in range(row)]) for k in range(1, row)
    ]
    return tuple(
        normalize(
            chunk_heads,
            [atts[c] for c in range(len(done_heads))],
            [raws[c] for c in range(len(done_heads))],
            all_sums,
            norm_gain,
            step_queries.shape[0],
            width * row,
        )
    )


def solution(mesh):
    return jax.shard_map(
        on_device,
        mesh=mesh,
        in_specs=(
            P("seq", "head"),
            P("seq", "head"),
            P("seq", "head"),
            P("seq", None, "head"),
            P("seq", None, "head"),
            P("seq"),
            P(None, "seq", "head"),
            P(None, "seq", "head"),
            P(None, "seq", "head"),
            P("head"),
        ),
        out_specs=(P("seq", "head"), P(None, "seq", "head")),
        check_vma=False,
    )
```

```python
import functools

import jax
import jax.numpy as jnp
from jax import lax
from jax.experimental import pallas as pl
from jax.experimental.pallas import tpu as pltpu
from jax.sharding import PartitionSpec as P

HEAD_DIM = 128
LANES = 128
F32 = jnp.float32
BF16 = jnp.bfloat16
VMEM_LIMIT = 24 * 1024 * 1024
SMEM = pl.BlockSpec(memory_space=pltpu.SMEM)
VMEM = pl.BlockSpec(memory_space=pltpu.VMEM)
ANY = pl.BlockSpec(memory_space=pl.ANY)


def dot(a, b, contract=((1,), (0,))):
    return lax.dot_general(a, b, (contract, ((), ())), preferred_element_type=F32)


def params():
    return pltpu.CompilerParams(vmem_limit_bytes=VMEM_LIMIT)


def cost(flops, moved):
    return pl.CostEstimate(flops=int(flops), bytes_accessed=int(moved), transcendentals=0)


def head_cols(head):
    return slice(head * HEAD_DIM, (head + 1) * HEAD_DIM)


def flat_rows(ref):
    return jnp.concatenate([ref[i].astype(F32) for i in range(ref.shape[0])], axis=0)


def place(group):
    rank = lax.axis_index("seq")
    return lax.rem(rank, group), lax.div(rank, group)


def owned_cols(group, m, each, heads):
    lo, hi = heads
    first = ((place(group)[0] ^ m) * each + lo) * HEAD_DIM
    return pl.ds(pl.multiple_of(first, HEAD_DIM), (hi - lo) * HEAD_DIM)


def split(x):
    high = x.astype(BF16)
    return high, (x - high.astype(F32)).astype(BF16)


def message(out_ref, rows, keys, values):
    for h in range(out_ref.shape[0]):
        cols = head_cols(h)
        out_ref[h, :HEAD_DIM, :] = dot(keys[:, cols], values[:, cols], ((0,), (0,)))
        out_ref[h, HEAD_DIM:, :] = rows[:, cols]


def step_rows(q_ref, cols):
    return jnp.concatenate([q_ref[i, :, cols].astype(F32) for i in range(q_ref.shape[0])], axis=0)


def fetched_state_kernel(group, m, each, heads, q_hbm, k_hbm, v_hbm, out_ref, q_buf, k_buf, v_buf, sems):
    cols = owned_cols(group, m, each, heads)
    copies = [
        pltpu.make_async_copy(k_hbm.at[:, cols], k_buf, sems.at[0]),
        pltpu.make_async_copy(v_hbm.at[:, cols], v_buf, sems.at[1]),
        pltpu.make_async_copy(q_hbm.at[:, :, cols], q_buf, sems.at[2]),
    ]
    for copy in copies:
        copy.start()
    for copy in copies:
        copy.wait()
    message(out_ref, step_rows(q_buf, slice(None)), k_buf[...], v_buf[...])


def fetched_states(m, group, each, heads, keys, values, step_queries):
    rows = keys.shape[0]
    steps, samples, _ = step_queries.shape
    count = heads[1] - heads[0]
    wide = count * HEAD_DIM
    hbm = pl.BlockSpec(memory_space=pltpu.HBM)
    return pl.pallas_call(
        functools.partial(fetched_state_kernel, group, m, each, heads),
        in_specs=[hbm, hbm, hbm],
        out_specs=VMEM,
        out_shape=jax.ShapeDtypeStruct((count, HEAD_DIM + steps * samples, HEAD_DIM), F32),
        scratch_shapes=[
            pltpu.VMEM((steps, samples, wide), step_queries.dtype),
            pltpu.VMEM((rows, wide), keys.dtype),
            pltpu.VMEM((rows, wide), values.dtype),
            pltpu.SemaphoreType.DMA((3,)),
        ],
        compiler_params=params(),
        cost_estimate=cost(2 * rows * wide * HEAD_DIM, 4 * rows * wide),
        name="fetched_states",
    )(
        pltpu.with_memory_space_constraint(step_queries, pltpu.HBM),
        pltpu.with_memory_space_constraint(keys, pltpu.HBM),
        pltpu.with_memory_space_constraint(values, pltpu.HBM),
    )


def state_kernel(group, owners, each, heads, q_ref, k_ref, v_ref, *refs):
    out_refs = refs[-len(owners) :]
    for m, out_ref in zip(owners, out_refs):
        cols = owned_cols(group, m, each, heads)
        message(out_ref, step_rows(q_ref, cols), k_ref[:, cols], v_ref[:, cols])


def block_states(owners, group, each, heads, keys, values, step_queries, after):
    rows = keys.shape[0]
    steps, samples, _ = step_queries.shape
    count = heads[1] - heads[0]
    wide = count * HEAD_DIM
    shape = jax.ShapeDtypeStruct((count, HEAD_DIM + steps * samples, HEAD_DIM), F32)
    return pl.pallas_call(
        functools.partial(state_kernel, group, owners, each, heads),
        in_specs=[VMEM, VMEM, VMEM] + [ANY] * len(after),
        out_specs=[VMEM] * len(owners),
        out_shape=[shape] * len(owners),
        compiler_params=params(),
        cost_estimate=cost(2 * rows * wide * HEAD_DIM * len(owners), 4 * rows * wide * len(owners)),
        name="block_states",
    )(step_queries, keys, values, *after)


def total_kernel(group, heads, *refs):
    here = slice(*heads)
    total = refs[0][here, :HEAD_DIM, :]
    for part in refs[1:group]:
        total = total + part[here, :HEAD_DIM, :]
    refs[-1][...] = total


def group_total(parts, heads, after):
    shape = (heads[1] - heads[0], HEAD_DIM, HEAD_DIM)
    return pl.pallas_call(
        functools.partial(total_kernel, len(parts), heads),
        in_specs=[VMEM] * len(parts) + [ANY] * len(after),
        out_specs=VMEM,
        out_shape=jax.ShapeDtypeStruct(shape, F32),
        compiler_params=params(),
        cost_estimate=cost(0, 4 * shape[0] * HEAD_DIM * HEAD_DIM * (len(parts) + 1)),
        name="group_total",
    )(*parts, *after)


def prior_kernel(owners, group, others, top, *refs):
    parts, total_ref = refs[:group], refs[group]
    other_refs, out_refs = refs[group + 1 : group + 1 + others], refs[-group:]
    here, block = place(group)
    for h in range(total_ref.shape[0]):
        entering = jnp.zeros((HEAD_DIM, HEAD_DIM), F32)
        final = total_ref[h]
        for k in range(others):
            other = other_refs[k][h]
            entering = entering + jnp.where(block > k, other, 0.0)
            final = final + other
        high, low = split(final)
        query = jnp.concatenate([part[top + h, HEAD_DIM:, :] for part in parts], axis=0)
        query = query.astype(BF16)
        raw = dot(query, high) + dot(query, low)
        dec = raw.shape[0] // group
        for m in range(group):
            out_ref = out_refs[owners.index(m)]
            prior = entering
            for k in range(group):
                if k != m:
                    prior = prior + jnp.where(
                        (here ^ k) < (here ^ m), parts[k][top + h, :HEAD_DIM, :], 0.0
                    )
            out_ref[h, :HEAD_DIM, :] = prior
            out_ref[h, HEAD_DIM:, :] = raw[m * dec : (m + 1) * dec]


def priors(owners, parts, top, total, others, after):
    group = len(parts)
    shape = (total.shape[0], *parts[0].shape[1:])
    return pl.pallas_call(
        functools.partial(prior_kernel, owners, group, len(others), top),
        in_specs=[VMEM] * (group + 1 + len(others)) + [ANY] * len(after),
        out_specs=[VMEM] * group,
        out_shape=[jax.ShapeDtypeStruct(shape, F32)] * group,
        compiler_params=params(),
        cost_estimate=cost(0, 4 * total.size * (2 * group + 1 + len(others))),
        name="priors",
    )(*parts, total, *others, *after)


def intra_kernel(tile, heads, q_ref, k_ref, v_ref, *refs):
    out_ref = refs[-1]
    rows, wide = out_ref.shape
    keep = lax.broadcasted_iota(jnp.int32, (tile, tile), 0) >= lax.broadcasted_iota(
        jnp.int32, (tile, tile), 1
    )
    for h, head in enumerate(heads):
        cols = head_cols(head)
        total = None
        for i in range(0, rows, tile):
            scores = dot(q_ref[i:, cols], k_ref[i : i + tile, cols], ((1,), (1,)))
            near = jnp.where(keep, scores[:tile], 0.0).astype(BF16)
            if i + tile < rows:
                near = jnp.concatenate([near, scores[tile:].astype(BF16)], axis=0)
            part = dot(near, v_ref[i : i + tile, cols])
            total = part if total is None else total + part
            out_ref[i : i + tile, head_cols(h)] = total[:tile]
            total = total[tile:]


def intra_block(heads, queries, keys, values, after):
    rows = queries.shape[0]
    wide = len(heads) * HEAD_DIM
    tile = 256 if rows % 256 == 0 else rows
    return pl.pallas_call(
        functools.partial(intra_kernel, tile, heads),
        in_specs=[VMEM] * 3 + [ANY] * len(after),
        out_specs=VMEM,
        out_shape=jax.ShapeDtypeStruct((rows, wide), F32),
        compiler_params=params(),
        cost_estimate=cost(4 * rows * rows * wide, 10 * rows * wide),
        name="intra_block",
    )(queries, keys, values, *after)


def suffix_kernel(lengths_ref, q_ref, k_ref, v_ref, sk_ref, sv_ref, *refs):
    out_ref = refs[-1]
    samples, suffix, width = k_ref.shape
    steps = q_ref.shape[0]
    rows = steps * samples
    tokens = samples * suffix
    heads = max(1, min(LANES // rows, width // HEAD_DIM))
    queries = flat_rows(q_ref)
    step_keys = flat_rows(sk_ref).astype(BF16)
    step_values = flat_rows(sv_ref).astype(BF16)

    at = lax.broadcasted_iota(jnp.int32, (heads * rows, tokens), 0) % samples
    token = lax.broadcasted_iota(jnp.int32, (heads * rows, tokens), 1)
    ends = jnp.zeros((heads * rows, tokens), jnp.int32)
    for n in range(samples):
        ends = jnp.where(at == n, n * suffix + lengths_ref[n], ends)
    live = (token >= at * suffix) & (token < ends)
    row = lax.broadcasted_iota(jnp.int32, (heads * rows, rows), 0) % rows
    col = lax.broadcasted_iota(jnp.int32, (heads * rows, rows), 1)
    near = (row % samples == col % samples) & (row // samples >= col // samples)

    pair = 2 if heads % 2 == 0 else 1
    wide = pair * HEAD_DIM
    for top in range(0, width // HEAD_DIM, heads):
        scores = jnp.zeros((tokens, heads * rows), F32)
        step_scores = jnp.zeros((rows, heads * rows), F32)
        for h in range(0, heads, pair):
            cols = slice((top + h) * HEAD_DIM, (top + h) * HEAD_DIM + wide)
            pieces = []
            for p in range(pair):
                own = [jnp.zeros((rows, HEAD_DIM), F32)] * pair
                own[p] = queries[:, head_cols(top + h + p)]
                pieces.append(jnp.concatenate(own, axis=1))
            if h:
                pieces.insert(0, jnp.zeros((h * rows, wide), F32))
            if h + pair < heads:
                pieces.append(jnp.zeros(((heads - pair - h) * rows, wide), F32))
            placed = jnp.concatenate(pieces, axis=0).astype(BF16)
            keys = k_ref[:, :, cols].reshape(tokens, wide)
            scores = scores + dot(keys, placed, ((1,), (1,)))
            step_scores = step_scores + dot(step_keys[:, cols], placed, ((1,), (1,)))
        halves = split(jnp.where(live, scores.T, 0.0))
        step_halves = split(jnp.where(near, step_scores.T, 0.0))
        for h in range(0, heads, pair):
            cols = slice((top + h) * HEAD_DIM, (top + h) * HEAD_DIM + wide)
            own = slice(h * rows, (h + pair) * rows)
            values = v_ref[:, :, cols].reshape(tokens, wide)
            both = dot(jnp.concatenate([x[own] for x in halves], axis=0), values) + dot(
                jnp.concatenate([x[own] for x in step_halves], axis=0), step_values[:, cols]
            )
            for p in range(pair):
                high = slice(p * rows, (p + 1) * rows)
                low = slice((pair + p) * rows, (pair + p + 1) * rows)
                out_ref[:, head_cols(top + h + p)] = both[high, head_cols(p)] + both[low, head_cols(p)]


def suffix_part(lengths, step_queries, suffix_keys, suffix_values, step_keys, step_values, after):
    samples, suffix, width = suffix_keys.shape
    steps = step_queries.shape[0]
    return pl.pallas_call(
        suffix_kernel,
        in_specs=[SMEM] + [VMEM] * 5 + [ANY] * len(after),
        out_specs=VMEM,
        out_shape=jax.ShapeDtypeStruct((steps * samples, width), F32),
        compiler_params=params(),
        cost_estimate=cost(64 * samples * suffix * width, 4 * samples * suffix * width),
        name="suffix_part",
    )(lengths, step_queries, suffix_keys, suffix_values, step_keys, step_values, *after)


def attended_kernel(group, owners, pieces, each, heads, first, last, q_ref, extra_ref, *refs):
    intra_refs, refs = refs[:pieces], refs[pieces:]
    parts = dict(zip(owners, refs))
    att_ref, raw_ref, sum_ref, acc_ref = refs[-4:]
    rows = q_ref.shape[0]
    dec = extra_ref.shape[0]
    count = heads[1] - heads[0]
    if first:
        acc_ref[...] = jnp.zeros_like(acc_ref)
    else:
        acc_ref[...] = refs[len(owners)][...]
    for m in owners:
        all_cols = owned_cols(group, m, each, heads)
        own_cols = owned_cols(group, m, count, (0, count))
        query = q_ref[:, all_cols]
        extra = extra_ref[:, all_cols]
        if pieces == 1:
            intra = intra_refs[0][:, own_cols]
        else:
            owner = place(group)[0] ^ m
            share = group // pieces
            at = pl.multiple_of(lax.rem(owner, share) * count * HEAD_DIM, HEAD_DIM)
            intra = intra_refs[0][:, pl.ds(at, count * HEAD_DIM)]
            for i in range(1, pieces):
                intra = jnp.where(
                    lax.div(owner, share) == i, intra_refs[i][:, pl.ds(at, count * HEAD_DIM)], intra
                )
        squares = acc_ref[:rows, :]
        raw_squares = acc_ref[rows : rows + dec, :]
        atts, raws = [], []
        for h in range(count):
            cols = head_cols(h)
            att = intra[:, cols] + dot(query[:, cols], parts[m][h, :HEAD_DIM, :].astype(BF16))
            raw = extra[:, cols] + parts[m][h, HEAD_DIM:, :]
            squares = squares + att * att
            raw_squares = raw_squares + raw * raw
            atts.append(att)
            raws.append(raw)
        att_ref[:, own_cols] = jnp.concatenate(atts, axis=1)
        raw_ref[:, own_cols] = jnp.concatenate(raws, axis=1)
        acc_ref[:rows, :] = squares
        acc_ref[rows : rows + dec, :] = raw_squares
    if last:
        sum_ref[...] = jnp.sum(acc_ref[...].T, axis=0, keepdims=True)
    else:
        sum_ref[...] = acc_ref[...]


def attend(owners, each, heads, last, queries, intra, extra, parts, before, begun):
    group = len(parts)
    parts = [parts[m] for m in owners]
    wide = group * (heads[1] - heads[0]) * HEAD_DIM
    rows, dec = queries.shape[0], extra.shape[0]
    pieces = len(intra)
    padded = -(-(rows + dec) // LANES) * LANES
    sums = (1, padded) if last else (padded, LANES)
    return pl.pallas_call(
        functools.partial(attended_kernel, group, owners, pieces, each, heads, not before, last),
        in_specs=[VMEM] * (2 + pieces + len(owners) + len(before) + len(begun)),
        out_specs=[VMEM] * 3,
        out_shape=[
            jax.ShapeDtypeStruct((rows, wide), F32),
            jax.ShapeDtypeStruct((dec, wide), F32),
            jax.ShapeDtypeStruct(sums, F32),
        ],
        scratch_shapes=[pltpu.VMEM((padded, LANES), F32)],
        compiler_params=params(),
        cost_estimate=cost(2 * rows * wide * HEAD_DIM, 10 * rows * wide),
        input_output_aliases={2 + pieces + len(owners) + len(before) + i: i for i in range(len(begun))},
        name="attend",
    )(queries, extra, *intra, *parts, *before, *begun)


def gain_kernel(heads, gain_ref, *refs):
    chunks = len(heads)
    for c in range(chunks):
        for h, head in enumerate(heads[c]):
            cols = head_cols(h)
            refs[chunks + c][:, cols] = refs[c][:, cols] * gain_ref[:, head_cols(head)]


def gained(heads, atts, gain):
    return pl.pallas_call(
        functools.partial(gain_kernel, heads),
        in_specs=[VMEM] * (1 + len(atts)),
        out_specs=[VMEM] * len(atts),
        out_shape=[jax.ShapeDtypeStruct(att.shape, F32) for att in atts],
        compiler_params=params(),
        cost_estimate=cost(0, 8 * sum(att.size for att in atts)),
        name="gained",
    )(gain[None, :], *atts)


def norm_kernel(heads, sums, width, tile, gain_ref, *refs):
    chunks = len(heads)
    sum_refs = refs[:sums]
    att_refs = refs[sums : sums + chunks]
    raw_refs = refs[sums + chunks : sums + 2 * chunks]
    out_hbm, dec_hbm, scale_ref, buf_ref, dec_ref, sems = refs[sums + 2 * chunks :]
    rows = att_refs[0].shape[0]
    dec = raw_refs[0].shape[0]
    samples = dec_ref.shape[1]
    total = sum_refs[0][...]
    for ref in sum_refs[1:]:
        total = total + ref[...]
    scale = lax.rsqrt(total / width + 1e-06)
    scale_ref[...] = jnp.broadcast_to(scale, (LANES, scale.shape[1])).T
    copies = []
    for i in range(rows // tile):
        here = slice(i * tile, (i + 1) * tile)
        row_scale = scale_ref[here, :]
        for c in range(chunks):
            for h, head in enumerate(heads[c]):
                at = head_cols(head)
                buf_ref[here, at] = (att_refs[c][here, head_cols(h)] * row_scale).astype(BF16)
        copies.append(pltpu.make_async_copy(buf_ref.at[here], out_hbm.at[here], sems.at[i]))
        copies[-1].start()
        if i == 0:
            row_scale = scale_ref[rows : rows + dec, :]
            for c in range(chunks):
                for h, head in enumerate(heads[c]):
                    at = head_cols(head)
                    out = raw_refs[c][:, head_cols(h)] * row_scale * gain_ref[:, at]
                    for j in range(dec_ref.shape[0]):
                        dec_ref[j, :, at] = out[j * samples : (j + 1) * samples].astype(BF16)
            copies.append(pltpu.make_async_copy(dec_ref, dec_hbm, sems.at[rows // tile]))
            copies[-1].start()
    for copy in copies:
        copy.wait()


def normalize(heads, atts, raws, sums, gain, steps, width_all):
    rows, width = atts[0].shape[0], gain.shape[0]
    dec = raws[0].shape[0]
    tile = 128 if rows % 128 == 0 else rows
    return pl.pallas_call(
        functools.partial(norm_kernel, heads, len(sums), width_all, tile),
        in_specs=[VMEM] * (1 + len(sums) + 2 * len(atts)),
        out_specs=[pl.BlockSpec(memory_space=pltpu.HBM)] * 2,
        out_shape=[
            jax.ShapeDtypeStruct((rows, width), BF16),
            jax.ShapeDtypeStruct((steps, dec // steps, width), BF16),
        ],
        scratch_shapes=[
            pltpu.VMEM((sums[0].shape[1], LANES), F32),
            pltpu.VMEM((rows, width), BF16),
            pltpu.VMEM((steps, dec // steps, width), BF16),
            pltpu.SemaphoreType.DMA((rows // tile + 1,)),
        ],
        compiler_params=params(),
        cost_estimate=cost(0, 6 * rows * width),
        name="normalize",
    )(gain[None, :], *sums, *atts, *raws)


SENT = (1, 1)
DONE = (1, 1)
ORDER = ("s0", "s1", "t0", "i0.0", "i0.1", "p0", "t1", "x", "p1", "i1", "a0", "a1")
PIECES = (2, 1)


def group_size(devices, heads):
    size = 1
    while devices % (2 * size) == 0 and size * size < devices and heads % (4 * size) == 0:
        size *= 2
    return size


def bounds(shares, heads):
    marks = [0]
    for i in range(len(shares)):
        marks.append(heads * sum(shares[: i + 1]) // sum(shares))
    return list(zip(marks[:-1], marks[1:]))


def on_device(
    queries,
    keys,
    values,
    suffix_keys,
    suffix_values,
    suffix_lengths,
    step_queries,
    step_keys,
    step_values,
    norm_gain,
):
    width = queries.shape[1]
    heads_here = width // HEAD_DIM
    devices = lax.axis_size("seq")
    group = group_size(devices, heads_here)
    blocks = devices // group
    each = heads_here // group
    fine = each % sum(DONE) == 0 and each % sum(SENT) == 0
    sent_heads, done_heads = (bounds(SENT, each), bounds(DONE, each)) if fine else (
        bounds((1, 1), each),
        bounds((1, 1), each),
    )
    chunk_heads = [
        [owner * each + h for owner in range(group) for h in range(lo, hi)] for lo, hi in done_heads
    ]

    def swap(messages):
        return [messages[0]] + [
            lax.ppermute(
                messages[m],
                "seq",
                [(i, i // group * group + (i % group ^ m)) for i in range(devices)],
            )
            for m in range(1, group)
        ]

    owners = list(range(group))[::-1]

    def ordered(owners, messages):
        made = dict(zip(owners, messages))
        return [made[m] for m in range(group)]

    def across(total):
        return [
            lax.ppermute(total, "seq", [(i, (i + k * group) % devices) for i in range(devices)])
            for k in range(1, blocks)
        ]

    def holder(c):
        lo, hi = done_heads[c]
        for i, (start, end) in enumerate(sent_heads):
            if start <= lo and hi <= end:
                return i, lo - start

    parts, totals, others, entering, intras, atts, raws = {}, {}, {}, {}, {}, {}, {}
    extra, sums, last = None, [], []
    for step in ORDER:
        kind, c = step[0], int(step[1:].split(".")[0] or 0) if len(step) > 1 else 0
        if kind == "s" and c < len(sent_heads):
            if c == 0:
                m = owners[0]
                given = (group, each, sent_heads[0], keys, values, step_queries)
                first = fetched_states(m, *given)
                rest = block_states([i for i in owners if i != m], *given, [first])
                messages = ordered([m] + [i for i in owners if i != m], [first, *rest])
                last = [rest[0]]
            else:
                messages = block_states(
                    owners,
                    group,
                    each,
                    sent_heads[c],
                    keys,
                    values,
                    step_queries,
                    last,
                )
                last = [messages[0]]
                messages = ordered(owners, messages)
            parts[c] = swap(messages)
        elif kind == "t" and c < len(done_heads):
            i, top = holder(c)
            count = done_heads[c][1] - done_heads[c][0]
            totals[c] = group_total(parts[i], (top, top + count), last)
            others[c] = across(totals[c])
            last = [totals[c]]
        elif kind == "p" and c < len(done_heads):
            i, top = holder(c)
            messages = priors(owners, parts[i], top, totals[c], others[c], last)
            entering[c] = swap(ordered(owners, messages))
            last = [messages[0]]
        elif kind == "i" and c < len(done_heads):
            heads = chunk_heads[c]
            if "." in step:
                share = len(heads) // PIECES[c]
                piece = int(step.split(".")[1])
                heads = heads[piece * share : (piece + 1) * share]
            intras.setdefault(c, []).append(intra_block(heads, queries, keys, values, last))
            last = [intras[c][-1]]
        elif kind == "x":
            extra = suffix_part(
                suffix_lengths,
                step_queries,
                suffix_keys,
                suffix_values,
                step_keys,
                step_values,
                last,
            )
            last = [extra]
        elif kind == "a" and c < len(done_heads):
            last_chunk = c == len(done_heads) - 1
            begun = []
            near = group // 2 if last_chunk else group
            for some in ([*range(near)], [*range(near, group)]):
                if some:
                    *begun, total = attend(
                        some,
                        each,
                        done_heads[c],
                        last_chunk and group - 1 in some,
                        queries,
                        intras[c],
                        extra,
                        entering[c],
                        sums,
                        begun,
                    )
                    sums = [total]
            atts[c], raws[c] = begun
    row = lax.axis_size("head")
    step = (lambda i, k: i ^ k) if row & (row - 1) == 0 else (lambda i, k: (i + k) % row)
    all_sums = sums + [
        lax.ppermute(sums[0], "head", [(i, step(i, k)) for i in range(row)]) for k in range(1, row)
    ]
    return tuple(
        normalize(
            chunk_heads,
            gained(chunk_heads, [atts[c] for c in range(len(done_heads))], norm_gain),
            [raws[c] for c in range(len(done_heads))],
            all_sums,
            norm_gain,
            step_queries.shape[0],
            width * row,
        )
    )


def solution(mesh):
    return jax.shard_map(
        on_device,
        mesh=mesh,
        in_specs=(
            P("seq", "head"),
            P("seq", "head"),
            P("seq", "head"),
            P("seq", None, "head"),
            P("seq", None, "head"),
            P("seq"),
            P(None, "seq", "head"),
            P(None, "seq", "head"),
            P(None, "seq", "head"),
            P("head"),
        ),
        out_specs=(P("seq", "head"), P(None, "seq", "head")),
        check_vma=False,
    )
```

```python
import functools

import jax
import jax.numpy as jnp
from jax import lax
from jax.experimental import pallas as pl
from jax.experimental.pallas import tpu as pltpu
from jax.sharding import PartitionSpec as P

HEAD_DIM = 128
LANES = 128
F32 = jnp.float32
BF16 = jnp.bfloat16
VMEM_LIMIT = 24 * 1024 * 1024
SMEM = pl.BlockSpec(memory_space=pltpu.SMEM)
VMEM = pl.BlockSpec(memory_space=pltpu.VMEM)
ANY = pl.BlockSpec(memory_space=pl.ANY)


def dot(a, b, contract=((1,), (0,))):
    return lax.dot_general(a, b, (contract, ((), ())), preferred_element_type=F32)


def params():
    return pltpu.CompilerParams(vmem_limit_bytes=VMEM_LIMIT)


def cost(flops, moved):
    return pl.CostEstimate(flops=int(flops), bytes_accessed=int(moved), transcendentals=0)


def head_cols(head):
    return slice(head * HEAD_DIM, (head + 1) * HEAD_DIM)


def flat_rows(ref):
    return jnp.concatenate([ref[i].astype(F32) for i in range(ref.shape[0])], axis=0)


def place(group):
    rank = lax.axis_index("seq")
    return lax.rem(rank, group), lax.div(rank, group)


def owned_cols(group, m, each, heads):
    lo, hi = heads
    first = ((place(group)[0] ^ m) * each + lo) * HEAD_DIM
    return pl.ds(pl.multiple_of(first, HEAD_DIM), (hi - lo) * HEAD_DIM)


def split(x):
    high = x.astype(BF16)
    return high, (x - high.astype(F32)).astype(BF16)


def message(out_ref, rows, keys, values):
    for h in range(out_ref.shape[0]):
        cols = head_cols(h)
        out_ref[h, :HEAD_DIM, :] = dot(keys[:, cols], values[:, cols], ((0,), (0,)))
        out_ref[h, HEAD_DIM:, :] = rows[:, cols]


def step_rows(q_ref, cols):
    return jnp.concatenate([q_ref[i, :, cols].astype(F32) for i in range(q_ref.shape[0])], axis=0)


def fetched_state_kernel(group, m, each, heads, q_hbm, k_hbm, v_hbm, out_ref, q_buf, k_buf, v_buf, sems):
    cols = owned_cols(group, m, each, heads)
    copies = [
        pltpu.make_async_copy(k_hbm.at[:, cols], k_buf, sems.at[0]),
        pltpu.make_async_copy(v_hbm.at[:, cols], v_buf, sems.at[1]),
        pltpu.make_async_copy(q_hbm.at[:, :, cols], q_buf, sems.at[2]),
    ]
    for copy in copies:
        copy.start()
    for copy in copies:
        copy.wait()
    message(out_ref, step_rows(q_buf, slice(None)), k_buf[...], v_buf[...])


def fetched_states(m, group, each, heads, keys, values, step_queries):
    rows = keys.shape[0]
    steps, samples, _ = step_queries.shape
    count = heads[1] - heads[0]
    wide = count * HEAD_DIM
    hbm = pl.BlockSpec(memory_space=pltpu.HBM)
    return pl.pallas_call(
        functools.partial(fetched_state_kernel, group, m, each, heads),
        in_specs=[hbm, hbm, hbm],
        out_specs=VMEM,
        out_shape=jax.ShapeDtypeStruct((count, HEAD_DIM + steps * samples, HEAD_DIM), F32),
        scratch_shapes=[
            pltpu.VMEM((steps, samples, wide), step_queries.dtype),
            pltpu.VMEM((rows, wide), keys.dtype),
            pltpu.VMEM((rows, wide), values.dtype),
            pltpu.SemaphoreType.DMA((3,)),
        ],
        compiler_params=params(),
        cost_estimate=cost(2 * rows * wide * HEAD_DIM, 4 * rows * wide),
        name="fetched_states",
    )(
        pltpu.with_memory_space_constraint(step_queries, pltpu.HBM),
        pltpu.with_memory_space_constraint(keys, pltpu.HBM),
        pltpu.with_memory_space_constraint(values, pltpu.HBM),
    )


def state_kernel(group, owners, each, heads, q_ref, k_ref, v_ref, *refs):
    out_refs = refs[-len(owners) :]
    for m, out_ref in zip(owners, out_refs):
        cols = owned_cols(group, m, each, heads)
        message(out_ref, step_rows(q_ref, cols), k_ref[:, cols], v_ref[:, cols])


def block_states(owners, group, each, heads, keys, values, step_queries, after):
    rows = keys.shape[0]
    steps, samples, _ = step_queries.shape
    count = heads[1] - heads[0]
    wide = count * HEAD_DIM
    shape = jax.ShapeDtypeStruct((count, HEAD_DIM + steps * samples, HEAD_DIM), F32)
    return pl.pallas_call(
        functools.partial(state_kernel, group, owners, each, heads),
        in_specs=[VMEM, VMEM, VMEM] + [ANY] * len(after),
        out_specs=[VMEM] * len(owners),
        out_shape=[shape] * len(owners),
        compiler_params=params(),
        cost_estimate=cost(2 * rows * wide * HEAD_DIM * len(owners), 4 * rows * wide * len(owners)),
        name="block_states",
    )(step_queries, keys, values, *after)


def total_kernel(group, heads, *refs):
    here = slice(*heads)
    total = refs[0][here, :HEAD_DIM, :]
    for part in refs[1:group]:
        total = total + part[here, :HEAD_DIM, :]
    refs[-1][...] = total


def group_total(parts, heads, after):
    shape = (heads[1] - heads[0], HEAD_DIM, HEAD_DIM)
    return pl.pallas_call(
        functools.partial(total_kernel, len(parts), heads),
        in_specs=[VMEM] * len(parts) + [ANY] * len(after),
        out_specs=VMEM,
        out_shape=jax.ShapeDtypeStruct(shape, F32),
        compiler_params=params(),
        cost_estimate=cost(0, 4 * shape[0] * HEAD_DIM * HEAD_DIM * (len(parts) + 1)),
        name="group_total",
    )(*parts, *after)


def prior_kernel(owners, group, others, top, *refs):
    parts, total_ref = refs[:group], refs[group]
    other_refs, out_refs = refs[group + 1 : group + 1 + others], refs[-group:]
    here, block = place(group)
    for h in range(total_ref.shape[0]):
        entering = jnp.zeros((HEAD_DIM, HEAD_DIM), F32)
        final = total_ref[h]
        for k in range(others):
            other = other_refs[k][h]
            entering = entering + jnp.where(block > k, other, 0.0)
            final = final + other
        high, low = split(final)
        query = jnp.concatenate([part[top + h, HEAD_DIM:, :] for part in parts], axis=0)
        query = query.astype(BF16)
        raw = dot(query, high) + dot(query, low)
        dec = raw.shape[0] // group
        for m in range(group):
            out_ref = out_refs[owners.index(m)]
            prior = entering
            for k in range(group):
                if k != m:
                    prior = prior + jnp.where(
                        (here ^ k) < (here ^ m), parts[k][top + h, :HEAD_DIM, :], 0.0
                    )
            out_ref[h, :HEAD_DIM, :] = prior
            out_ref[h, HEAD_DIM:, :] = raw[m * dec : (m + 1) * dec]


def priors(owners, parts, top, total, others, after):
    group = len(parts)
    shape = (total.shape[0], *parts[0].shape[1:])
    return pl.pallas_call(
        functools.partial(prior_kernel, owners, group, len(others), top),
        in_specs=[VMEM] * (group + 1 + len(others)) + [ANY] * len(after),
        out_specs=[VMEM] * group,
        out_shape=[jax.ShapeDtypeStruct(shape, F32)] * group,
        compiler_params=params(),
        cost_estimate=cost(0, 4 * total.size * (2 * group + 1 + len(others))),
        name="priors",
    )(*parts, total, *others, *after)


def intra_kernel(tile, heads, q_ref, k_ref, v_ref, *refs):
    out_ref = refs[-1]
    rows, wide = out_ref.shape
    keep = lax.broadcasted_iota(jnp.int32, (tile, tile), 0) >= lax.broadcasted_iota(
        jnp.int32, (tile, tile), 1
    )
    for h, head in enumerate(heads):
        cols = head_cols(head)
        total = None
        for i in range(0, rows, tile):
            scores = dot(q_ref[i:, cols], k_ref[i : i + tile, cols], ((1,), (1,)))
            near = jnp.where(keep, scores[:tile], 0.0).astype(BF16)
            if i + tile < rows:
                near = jnp.concatenate([near, scores[tile:].astype(BF16)], axis=0)
            part = dot(near, v_ref[i : i + tile, cols])
            total = part if total is None else total + part
            out_ref[i : i + tile, head_cols(h)] = total[:tile]
            total = total[tile:]


def intra_block(heads, queries, keys, values, after):
    rows = queries.shape[0]
    wide = len(heads) * HEAD_DIM
    tile = 256 if rows % 256 == 0 else rows
    return pl.pallas_call(
        functools.partial(intra_kernel, tile, heads),
        in_specs=[VMEM] * 3 + [ANY] * len(after),
        out_specs=VMEM,
        out_shape=jax.ShapeDtypeStruct((rows, wide), F32),
        compiler_params=params(),
        cost_estimate=cost(4 * rows * rows * wide, 10 * rows * wide),
        name="intra_block",
    )(queries, keys, values, *after)


def suffix_kernel(lengths_ref, q_ref, k_ref, v_ref, sk_ref, sv_ref, *refs):
    out_ref = refs[-1]
    samples, suffix, width = k_ref.shape
    steps = q_ref.shape[0]
    rows = steps * samples
    tokens = samples * suffix
    heads = max(1, min(LANES // rows, width // HEAD_DIM))
    queries = flat_rows(q_ref)
    step_keys = flat_rows(sk_ref).astype(BF16)
    step_values = flat_rows(sv_ref).astype(BF16)

    at = lax.broadcasted_iota(jnp.int32, (heads * rows, tokens), 0) % samples
    token = lax.broadcasted_iota(jnp.int32, (heads * rows, tokens), 1)
    ends = jnp.zeros((heads * rows, tokens), jnp.int32)
    for n in range(samples):
        ends = jnp.where(at == n, n * suffix + lengths_ref[n], ends)
    live = (token >= at * suffix) & (token < ends)
    row = lax.broadcasted_iota(jnp.int32, (heads * rows, rows), 0) % rows
    col = lax.broadcasted_iota(jnp.int32, (heads * rows, rows), 1)
    near = (row % samples == col % samples) & (row // samples >= col // samples)

    pair = 2 if heads % 2 == 0 else 1
    wide = pair * HEAD_DIM
    for top in range(0, width // HEAD_DIM, heads):
        scores = jnp.zeros((tokens, heads * rows), F32)
        step_scores = jnp.zeros((rows, heads * rows), F32)
        for h in range(0, heads, pair):
            cols = slice((top + h) * HEAD_DIM, (top + h) * HEAD_DIM + wide)
            pieces = []
            for p in range(pair):
                own = [jnp.zeros((rows, HEAD_DIM), F32)] * pair
                own[p] = queries[:, head_cols(top + h + p)]
                pieces.append(jnp.concatenate(own, axis=1))
            if h:
                pieces.insert(0, jnp.zeros((h * rows, wide), F32))
            if h + pair < heads:
                pieces.append(jnp.zeros(((heads - pair - h) * rows, wide), F32))
            placed = jnp.concatenate(pieces, axis=0).astype(BF16)
            keys = k_ref[:, :, cols].reshape(tokens, wide)
            scores = scores + dot(keys, placed, ((1,), (1,)))
            step_scores = step_scores + dot(step_keys[:, cols], placed, ((1,), (1,)))
        halves = split(jnp.where(live, scores.T, 0.0))
        step_halves = split(jnp.where(near, step_scores.T, 0.0))
        for h in range(0, heads, pair):
            cols = slice((top + h) * HEAD_DIM, (top + h) * HEAD_DIM + wide)
            own = slice(h * rows, (h + pair) * rows)
            values = v_ref[:, :, cols].reshape(tokens, wide)
            both = dot(jnp.concatenate([x[own] for x in halves], axis=0), values) + dot(
                jnp.concatenate([x[own] for x in step_halves], axis=0), step_values[:, cols]
            )
            for p in range(pair):
                high = slice(p * rows, (p + 1) * rows)
                low = slice((pair + p) * rows, (pair + p + 1) * rows)
                out_ref[:, head_cols(top + h + p)] = both[high, head_cols(p)] + both[low, head_cols(p)]


def suffix_part(lengths, step_queries, suffix_keys, suffix_values, step_keys, step_values, after):
    samples, suffix, width = suffix_keys.shape
    steps = step_queries.shape[0]
    return pl.pallas_call(
        suffix_kernel,
        in_specs=[SMEM] + [VMEM] * 5 + [ANY] * len(after),
        out_specs=VMEM,
        out_shape=jax.ShapeDtypeStruct((steps * samples, width), F32),
        compiler_params=params(),
        cost_estimate=cost(64 * samples * suffix * width, 4 * samples * suffix * width),
        name="suffix_part",
    )(lengths, step_queries, suffix_keys, suffix_values, step_keys, step_values, *after)


def attended_kernel(group, owners, pieces, each, heads, first, last, q_ref, extra_ref, *refs):
    intra_refs, refs = refs[:pieces], refs[pieces:]
    parts = dict(zip(owners, refs))
    att_ref, raw_ref, sum_ref, acc_ref = refs[-4:]
    rows = q_ref.shape[0]
    dec = extra_ref.shape[0]
    count = heads[1] - heads[0]
    if first:
        acc_ref[...] = jnp.zeros_like(acc_ref)
    else:
        acc_ref[...] = refs[len(owners)][...]
    for m in owners:
        all_cols = owned_cols(group, m, each, heads)
        own_cols = owned_cols(group, m, count, (0, count))
        query = q_ref[:, all_cols]
        extra = extra_ref[:, all_cols]
        if pieces == 1:
            intra = intra_refs[0][:, own_cols]
        else:
            owner = place(group)[0] ^ m
            share = group // pieces
            at = pl.multiple_of(lax.rem(owner, share) * count * HEAD_DIM, HEAD_DIM)
            intra = intra_refs[0][:, pl.ds(at, count * HEAD_DIM)]
            for i in range(1, pieces):
                intra = jnp.where(
                    lax.div(owner, share) == i, intra_refs[i][:, pl.ds(at, count * HEAD_DIM)], intra
                )
        squares = acc_ref[:rows, :]
        raw_squares = acc_ref[rows : rows + dec, :]
        atts, raws = [], []
        for h in range(count):
            cols = head_cols(h)
            att = intra[:, cols] + dot(query[:, cols], parts[m][h, :HEAD_DIM, :].astype(BF16))
            raw = extra[:, cols] + parts[m][h, HEAD_DIM:, :]
            squares = squares + att * att
            raw_squares = raw_squares + raw * raw
            atts.append(att)
            raws.append(raw)
        att_ref[:, own_cols] = jnp.concatenate(atts, axis=1)
        raw_ref[:, own_cols] = jnp.concatenate(raws, axis=1)
        acc_ref[:rows, :] = squares
        acc_ref[rows : rows + dec, :] = raw_squares
    if last:
        sum_ref[...] = jnp.sum(acc_ref[...].T, axis=0, keepdims=True)
    else:
        sum_ref[...] = acc_ref[...]


def attend(owners, each, heads, last, queries, intra, extra, parts, before, begun):
    group = len(parts)
    parts = [parts[m] for m in owners]
    wide = group * (heads[1] - heads[0]) * HEAD_DIM
    rows, dec = queries.shape[0], extra.shape[0]
    pieces = len(intra)
    padded = -(-(rows + dec) // LANES) * LANES
    sums = (1, padded) if last else (padded, LANES)
    return pl.pallas_call(
        functools.partial(attended_kernel, group, owners, pieces, each, heads, not before, last),
        in_specs=[VMEM] * (2 + pieces + len(owners) + len(before) + len(begun)),
        out_specs=[VMEM] * 3,
        out_shape=[
            jax.ShapeDtypeStruct((rows, wide), F32),
            jax.ShapeDtypeStruct((dec, wide), F32),
            jax.ShapeDtypeStruct(sums, F32),
        ],
        scratch_shapes=[pltpu.VMEM((padded, LANES), F32)],
        compiler_params=params(),
        cost_estimate=cost(2 * rows * wide * HEAD_DIM, 10 * rows * wide),
        input_output_aliases={2 + pieces + len(owners) + len(before) + i: i for i in range(len(begun))},
        name="attend",
    )(queries, extra, *intra, *parts, *before, *begun)


def gain_kernel(heads, gain_ref, *refs):
    chunks = len(heads)
    for c in range(chunks):
        for h, head in enumerate(heads[c]):
            cols = head_cols(h)
            refs[chunks + c][:, cols] = refs[c][:, cols] * gain_ref[:, head_cols(head)]


def gained(heads, atts, gain):
    return pl.pallas_call(
        functools.partial(gain_kernel, heads),
        in_specs=[VMEM] * (1 + len(atts)),
        out_specs=[VMEM] * len(atts),
        out_shape=[jax.ShapeDtypeStruct(att.shape, F32) for att in atts],
        compiler_params=params(),
        cost_estimate=cost(0, 8 * sum(att.size for att in atts)),
        name="gained",
    )(gain[None, :], *atts)


def norm_kernel(heads, sums, width, tile, gain_ref, *refs):
    chunks = len(heads)
    sum_refs = refs[:sums]
    att_refs = refs[sums : sums + chunks]
    raw_refs = refs[sums + chunks : sums + 2 * chunks]
    out_hbm, dec_hbm, scale_ref, buf_ref, dec_ref, sems = refs[sums + 2 * chunks :]
    rows = att_refs[0].shape[0]
    dec = raw_refs[0].shape[0]
    samples = dec_ref.shape[1]
    total = sum_refs[0][...]
    for ref in sum_refs[1:]:
        total = total + ref[...]
    scale = lax.rsqrt(total / width + 1e-06)
    scale_ref[...] = jnp.broadcast_to(scale, (LANES, scale.shape[1])).T
    copies = []
    for i in range(rows // tile):
        here = slice(i * tile, (i + 1) * tile)
        row_scale = scale_ref[here, :]
        for c in range(chunks):
            for h, head in enumerate(heads[c]):
                at = head_cols(head)
                buf_ref[here, at] = (att_refs[c][here, head_cols(h)] * row_scale).astype(BF16)
        copies.append(pltpu.make_async_copy(buf_ref.at[here], out_hbm.at[here], sems.at[i]))
        copies[-1].start()
        if i == 0:
            row_scale = scale_ref[rows : rows + dec, :]
            for c in range(chunks):
                for h, head in enumerate(heads[c]):
                    at = head_cols(head)
                    out = raw_refs[c][:, head_cols(h)] * row_scale * gain_ref[:, at]
                    for j in range(dec_ref.shape[0]):
                        dec_ref[j, :, at] = out[j * samples : (j + 1) * samples].astype(BF16)
            copies.append(pltpu.make_async_copy(dec_ref, dec_hbm, sems.at[rows // tile]))
            copies[-1].start()
    for copy in copies:
        copy.wait()


def normalize(heads, atts, raws, sums, gain, steps, width_all):
    rows, width = atts[0].shape[0], gain.shape[0]
    dec = raws[0].shape[0]
    tile = 128 if rows % 128 == 0 else rows
    return pl.pallas_call(
        functools.partial(norm_kernel, heads, len(sums), width_all, tile),
        in_specs=[VMEM] * (1 + len(sums) + 2 * len(atts)),
        out_specs=[pl.BlockSpec(memory_space=pltpu.HBM)] * 2,
        out_shape=[
            jax.ShapeDtypeStruct((rows, width), BF16),
            jax.ShapeDtypeStruct((steps, dec // steps, width), BF16),
        ],
        scratch_shapes=[
            pltpu.VMEM((sums[0].shape[1], LANES), F32),
            pltpu.VMEM((rows, width), BF16),
            pltpu.VMEM((steps, dec // steps, width), BF16),
            pltpu.SemaphoreType.DMA((rows // tile + 1,)),
        ],
        compiler_params=params(),
        cost_estimate=cost(0, 6 * rows * width),
        name="normalize",
    )(gain[None, :], *sums, *atts, *raws)


SENT = (1, 1)
DONE = (1, 1)
ORDER = ("s0", "s1", "t0", "i0.0", "i0.1", "p0", "t1", "x", "p1", "i1", "a0", "a1")
PIECES = (2, 1)


def group_size(devices, heads):
    size = 1
    while devices % (2 * size) == 0 and size * size < devices and heads % (4 * size) == 0:
        size *= 2
    return size


def bounds(shares, heads):
    marks = [0]
    for i in range(len(shares)):
        marks.append(heads * sum(shares[: i + 1]) // sum(shares))
    return list(zip(marks[:-1], marks[1:]))


def on_device(
    queries,
    keys,
    values,
    suffix_keys,
    suffix_values,
    suffix_lengths,
    step_queries,
    step_keys,
    step_values,
    norm_gain,
):
    width = queries.shape[1]
    heads_here = width // HEAD_DIM
    devices = lax.axis_size("seq")
    group = group_size(devices, heads_here)
    blocks = devices // group
    each = heads_here // group
    fine = each % sum(DONE) == 0 and each % sum(SENT) == 0
    sent_heads, done_heads = (bounds(SENT, each), bounds(DONE, each)) if fine else (
        bounds((1, 1), each),
        bounds((1, 1), each),
    )
    chunk_heads = [
        [owner * each + h for owner in range(group) for h in range(lo, hi)] for lo, hi in done_heads
    ]

    def swap(messages):
        return [messages[0]] + [
            lax.ppermute(
                messages[m],
                "seq",
                [(i, i // group * group + (i % group ^ m)) for i in range(devices)],
            )
            for m in range(1, group)
        ]

    owners = list(range(group))[::-1]

    def ordered(owners, messages):
        made = dict(zip(owners, messages))
        return [made[m] for m in range(group)]

    def across(total):
        return [
            lax.ppermute(total, "seq", [(i, (i + k * group) % devices) for i in range(devices)])
            for k in range(1, blocks)
        ]

    def holder(c):
        lo, hi = done_heads[c]
        for i, (start, end) in enumerate(sent_heads):
            if start <= lo and hi <= end:
                return i, lo - start

    parts, totals, others, entering, intras, atts, raws = {}, {}, {}, {}, {}, {}, {}
    extra, sums, last = None, [], []
    for step in ORDER:
        kind, c = step[0], int(step[1:].split(".")[0] or 0) if len(step) > 1 else 0
        if kind == "s" and c < len(sent_heads):
            if c == 0:
                m = owners[0]
                given = (group, each, sent_heads[0], keys, values, step_queries)
                first = fetched_states(m, *given)
                rest = block_states([i for i in owners if i != m], *given, [first])
                messages = ordered([m] + [i for i in owners if i != m], [first, *rest])
                last = [rest[0]]
            else:
                messages = block_states(
                    owners,
                    group,
                    each,
                    sent_heads[c],
                    keys,
                    values,
                    step_queries,
                    last,
                )
                last = [messages[0]]
                messages = ordered(owners, messages)
            parts[c] = swap(messages)
        elif kind == "t" and c < len(done_heads):
            i, top = holder(c)
            count = done_heads[c][1] - done_heads[c][0]
            totals[c] = group_total(parts[i], (top, top + count), last)
            others[c] = across(totals[c])
            last = [totals[c]]
        elif kind == "p" and c < len(done_heads):
            i, top = holder(c)
            messages = priors(owners, parts[i], top, totals[c], others[c], last)
            entering[c] = swap(ordered(owners, messages))
            last = [messages[0]]
        elif kind == "i" and c < len(done_heads):
            heads = chunk_heads[c]
            if "." in step:
                share = len(heads) // PIECES[c]
                piece = int(step.split(".")[1])
                heads = heads[piece * share : (piece + 1) * share]
            intras.setdefault(c, []).append(intra_block(heads, queries, keys, values, last))
            last = [intras[c][-1]]
        elif kind == "x":
            extra = suffix_part(
                suffix_lengths,
                step_queries,
                suffix_keys,
                suffix_values,
                step_keys,
                step_values,
                last,
            )
            last = [extra]
        elif kind == "a" and c < len(done_heads):
            last_chunk = c == len(done_heads) - 1
            begun = []
            near = group - 1 if last_chunk else group
            for some in ([*range(near)], [*range(near, group)]):
                if some:
                    *begun, total = attend(
                        some,
                        each,
                        done_heads[c],
                        last_chunk and group - 1 in some,
                        queries,
                        intras[c],
                        extra,
                        entering[c],
                        sums,
                        begun,
                    )
                    sums = [total]
            atts[c], raws[c] = begun
    row = lax.axis_size("head")
    step = (lambda i, k: i ^ k) if row & (row - 1) == 0 else (lambda i, k: (i + k) % row)
    all_sums = sums + [
        lax.ppermute(sums[0], "head", [(i, step(i, k)) for i in range(row)]) for k in range(1, row)
    ]
    return tuple(
        normalize(
            chunk_heads,
            gained(chunk_heads, [atts[c] for c in range(len(done_heads))], norm_gain),
            [raws[c] for c in range(len(done_heads))],
            all_sums,
            norm_gain,
            step_queries.shape[0],
            width * row,
        )
    )


def solution(mesh):
    return jax.shard_map(
        on_device,
        mesh=mesh,
        in_specs=(
            P("seq", "head"),
            P("seq", "head"),
            P("seq", "head"),
            P("seq", None, "head"),
            P("seq", None, "head"),
            P("seq"),
            P(None, "seq", "head"),
            P(None, "seq", "head"),
            P(None, "seq", "head"),
            P("head"),
        ),
        out_specs=(P("seq", "head"), P(None, "seq", "head")),
        check_vma=False,
    )
```
